128 devices in a mesh: shot: 16 (over x_lo, z, core), node: 8 (over y, x_hi).
Axes of the slice: x: 4 (x_hi: 2, x_lo: 2; x = x_hi * 2 + x_lo), y: 4, z: 4, core: 2. Of those that a mesh axis runs over, the one named last changes fastest.
Arguments:
- up_time: bfloat16 [1024, 512, 1024], P(None, 'shot', 'node'), may hold values from -1 to 1
- downgoing: float32 [4, 2, 1024, 1024], P(None, None, 'shot', 'node'), may hold values from -0.1875 to 0.1875
- freq_idx: int32 [4], replicated, may hold values from 1 to 255
- node_map: int32 [1024], P('node'), may hold values from 0 to 127, as said below
Outputs:
- reflectivity: float32 [4, 2, 1024, 1024], P(None, None, None, 'node')
- residual: float32 [4, 2, 1024, 1024], P(None, None, 'shot', 'node')
The draws below stay inside these ranges and needn't reach their ends.
Inputs may be any that keep to these rules, and one draw needn't show every extreme that they name: `node_map`: within each aligned block of 128 nodes the slots are a permutation of 0 to 127.
All inputs are finite; a program needn't handle non-finite values.
Results may differ from the reference program's by a relative error of at most 0.0023.
Values may be sent and summed in bfloat16 or wider, within the bound.
No kernel may reach another device: no remote copies, remote signals or barrier semaphores. Data moves between devices by JAX's collectives and lax.ppermute only.
A program may use at most 128 MiB of HBM per device.

```python
import math
import jax
import jax.numpy as jnp
from jax import lax

NODES = 1024
NT = 512
F = 4
ITERS = 2
S_DEV = 64
SHOTS = 1024
NODE_DEV = 128
N_SHOT = 16


def draw_node_map(key, part):
    key = jax.random.fold_in(key, 7)
    subkeys = jax.random.split(key, NODES // NODE_DEV)
    permuted = jax.vmap(lambda sub: jax.random.permutation(sub, NODE_DEV))(subkeys)
    return permuted.reshape(NODES).astype(jnp.int32)


def place_ends(array, own_key, low, largest):
    extent = array.shape
    index_at = [jax.random.randint(jax.random.fold_in(own_key, axis), (), 0, extent[axis]) for axis in range(len(extent))]
    array = array.at[tuple(index_at)].set(low)
    longest = extent.index(max(extent))
    index_at[longest] = (index_at[longest] + 1) % extent[longest]
    return array.at[tuple(index_at)].set(largest)


def steps_of(stream_key, shape, cuts, smallest, high):
    def one(position, shards_of):
        heights = jax.random.uniform(jax.random.fold_in(jax.random.fold_in(stream_key, 6), position), (shards_of,), jnp.float32, smallest / len(cuts), high / len(cuts))
        return jnp.repeat(jnp.exp(heights), shape[position] // shards_of).reshape((-1,) + (1,) * (len(shape) - position - 1))

    factor_of = one(*cuts[0])
    for cut in cuts[1:]:
        factor_of = factor_of * one(*cut)
    return factor_of


def gaussian(rng, extent, spread, bound, cuts=(), held_as=jnp.bfloat16):
    entries = jax.random.normal(rng, extent, jnp.float32) * spread
    if len(cuts) > 0:
        entries = steps_of(rng, extent, cuts, -0.22, 0.18) * entries
    return jnp.clip(entries, min=-bound, max=bound).astype(held_as)


def setup_inputs(seed: int = 0) -> dict:
    seeds = jax.random.split(jax.random.key(seed), 5)
    up_time = gaussian(seeds[0], (SHOTS, NT, NODES), 0.0625, 1.0, ((1, 16), (2, 8)))
    downgoing = gaussian(seeds[1], (F, 2, SHOTS, NODES), SHOTS ** -0.5, 0.1875, ((2, 16), (3, 8)), jnp.float32)
    freq_idx = place_ends(jax.random.randint(seeds[2], (F,), 1, NT // 2), jax.random.fold_in(seeds[2], 1), 1, (NT // 2) - 1).astype(jnp.int32)
    node_map = draw_node_map(jax.random.fold_in(seeds[4], 71), 0)
    return {"up_time": up_time, "downgoing": downgoing, "freq_idx": freq_idx, "node_map": node_map}


MAXIMUM_ACCURACY = lax.Precision.HIGHEST


def dft_table(freq_idx, first_sample, sample_count):
    sample_index = first_sample + jnp.arange(sample_count, dtype=jnp.int32)
    product = (freq_idx[:, None] * sample_index[None, :]) % NT
    phase_angle = product.astype(jnp.float32) * (2.0 * math.pi / NT)
    stacked = jnp.stack([jnp.cos(phase_angle), -jnp.sin(phase_angle)], axis=1)
    return stacked.reshape(2 * F, sample_count).astype(jnp.bfloat16)


def forward(full_down, field):
    downward_real, downward_imaginary = full_down[:, 0], full_down[:, 1]
    wavefield_real, wavefield_imaginary = field[:, 0], field[:, 1]
    output_real = jnp.einsum('ylt,ytz->ylz', downward_real, wavefield_real, precision=MAXIMUM_ACCURACY) - jnp.einsum('ylt,ytz->ylz', downward_imaginary, wavefield_imaginary, precision=MAXIMUM_ACCURACY)
    output_imaginary = jnp.einsum('ylt,ytz->ylz', downward_real, wavefield_imaginary, precision=MAXIMUM_ACCURACY) + jnp.einsum('ylt,ytz->ylz', downward_imaginary, wavefield_real, precision=MAXIMUM_ACCURACY)
    return jnp.stack([output_real, output_imaginary], axis=1)


def adjoint(full_down, data):
    downward_real, downward_imaginary = full_down[:, 0], full_down[:, 1]
    data_real_part, data_imaginary = data[:, 0], data[:, 1]
    output_real = jnp.einsum('ujc,ujq->ucq', downward_real, data_real_part, precision=MAXIMUM_ACCURACY) + jnp.einsum('ujc,ujq->ucq', downward_imaginary, data_imaginary, precision=MAXIMUM_ACCURACY)
    output_imaginary = jnp.einsum('ujc,ujq->ucq', downward_real, data_imaginary, precision=MAXIMUM_ACCURACY) - jnp.einsum('ujc,ujq->ucq', downward_imaginary, data_real_part, precision=MAXIMUM_ACCURACY)
    return jnp.stack([output_real, output_imaginary], axis=1)


def symmetrize(field):
    return (field + jnp.swapaxes(field, 2, 3)) * 0.5


def squares(field):
    return jnp.sum(field * field, axis=(1, 2, 3))


def expand(values):
    return values[:, None, None, None]


def reference(up_time, downgoing, freq_idx, node_map):
    table = dft_table(freq_idx, 0, NT).astype(jnp.float32)
    trace_blocks = up_time.reshape(N_SHOT, S_DEV, NT, NODES)

    def transform(trace_block):
        return jnp.einsum('ft,stn->fsn', table, trace_block.astype(jnp.float32), precision=MAXIMUM_ACCURACY)

    spectra = lax.map(transform, trace_blocks)
    recorded = jnp.transpose(spectra, (1, 0, 2, 3)).reshape(F, 2, SHOTS, NODES)
    target = (jnp.arange(NODES, dtype=jnp.int32) // NODE_DEV) * NODE_DEV + node_map.astype(jnp.int32)
    upgoing = jnp.zeros_like(recorded).at[:, :, :, target].set(recorded)
    reflectivity = jnp.zeros((F, 2, NODES, NODES), jnp.float32)
    residual = upgoing
    gradient = symmetrize(adjoint(downgoing, residual))
    direction = gradient
    grad_norm = squares(gradient)
    for iteration in range(ITERS):
        image = forward(downgoing, direction)
        curvature = squares(image)
        step_size = expand(grad_norm / curvature)
        reflectivity = reflectivity + step_size * direction
        residual = residual - step_size * image
        if iteration + 1 < ITERS:
            gradient = symmetrize(adjoint(downgoing, residual))
            new_norm = squares(gradient)
            direction = gradient + expand(new_norm / grad_norm) * direction
            grad_norm = new_norm
    return reflectivity, residual
```

```python
import math

import jax
import jax.numpy as jnp
from jax import lax
from jax.sharding import Mesh, PartitionSpec as P

NODES = 1024
NT = 512
F = 4
SHOT = ("xl", "z", "core")
NODE = ("y", "xh")
PLANE = ("y", "xh", "xl", "core")
HIGH = lax.Precision.HIGH


def local_table(freq_idx, first, count):
    sample = first + jnp.arange(count, dtype=jnp.int32)
    product = freq_idx[:, None] * sample[None, :] % NT
    angle = product.astype(jnp.float32) * (2.0 * math.pi / NT)
    stacked = jnp.stack([jnp.cos(angle), -jnp.sin(angle)], axis=1)
    return stacked.reshape(2 * F, count).astype(jnp.bfloat16)


def mm(a, b):
    return lax.dot_general(a, b, (((1,), (0,)), ((), ())), precision=HIGH)


def mt(a, b):
    return lax.dot_general(a, b, (((1,), (1,)), ((), ())), precision=HIGH)


def adjoint_t(down, data):
    w = data.shape[1]
    both = data.reshape(2 * w, -1)
    with_real, with_imag = mm(both, down[0]), mm(both, down[1])
    return jnp.stack([with_real[:w] + with_imag[w:], with_real[w:] - with_imag[:w]])


def forward_t(down, field):
    w = field.shape[1]
    both = field.reshape(2 * w, -1)
    with_real, with_imag = mt(both, down[0]), mt(both, down[1])
    return jnp.stack([with_real[:w] - with_imag[w:], with_real[w:] + with_imag[:w]])


def symmetrize_t(field):
    w = field.shape[1]
    out = field.reshape(2, w, -1, w).transpose(2, 0, 3, 1)
    back = lax.all_to_all(out, PLANE, 0, 0, tiled=True)
    return (field + back.transpose(1, 2, 0, 3).reshape(field.shape)) * 0.5


def plane_sum(values):
    row = jnp.broadcast_to(jnp.stack(values)[None, :, None], (32, len(values), 128))
    return lax.all_to_all(row, PLANE, 0, 0, tiled=True).sum(0)[:, 0]


def dot(a, b):
    return jnp.sum(a * b)


def shards(up_time, downgoing, freq_idx, node_map):
    own = lax.all_to_all(downgoing, "z", 0, 0, tiled=True).transpose(1, 0, 2, 3)
    gathered = lax.all_gather(own.reshape(512, 128), PLANE, axis=0, tiled=True)
    down = gathered.reshape(8, 2, 2, 2, 4, 64, 128).transpose(3, 1, 4, 2, 5, 0, 6)
    down = down.reshape(2, NODES, NODES)

    count = up_time.shape[1]
    table = local_table(freq_idx, lax.axis_index(SHOT) * count, count)
    partial = jnp.einsum("ft,stn->fsn", table, up_time, preferred_element_type=jnp.float32)
    onehot = (node_map[:, None] == jnp.arange(128, dtype=jnp.int32)[None, :]).astype(jnp.float32)
    partial = jnp.einsum("fsm,mj->fjs", partial, onehot, precision=lax.Precision.HIGHEST)
    pieces = partial.reshape(F, 2, 2, 2, 32, 1024).transpose(2, 0, 3, 1, 4, 5)
    received = lax.all_to_all(pieces.reshape(16, 64, 1024), SHOT, 0, 0, tiled=True)
    data = received.sum(0).reshape(2, 32, 1024)

    gradient = symmetrize_t(adjoint_t(down, data))
    image = forward_t(down, gradient)
    again = symmetrize_t(adjoint_t(down, image))
    norm, curvature = plane_sum([dot(gradient, gradient), dot(image, image)])
    step = norm / curvature
    new_gradient = gradient - step * again
    change = image - step * forward_t(down, again)
    new_norm, change_change, change_image = plane_sum(
        [dot(new_gradient, new_gradient), dot(change, change), dot(change, image)]
    )
    beta = new_norm / norm
    new_curvature = change_change + 2.0 * beta * change_image + beta * beta * curvature
    new_step = new_norm / new_curvature
    result = step * gradient + new_step * (new_gradient + beta * gradient)
    residual = data - step * image - new_step * (change + beta * image)

    full = lax.all_gather(result.reshape(1, 64, 1024), SHOT, axis=0, tiled=True)
    full = full.reshape(2, F, 2, 2, 32, 1024).transpose(1, 3, 5, 0, 2, 4)
    out = residual.reshape(2, 32, 16, 64).transpose(2, 0, 3, 1)
    out = lax.all_to_all(out, SHOT, 0, 0, tiled=True)
    out = out.reshape(2, F, 2, 2, 64, 32).transpose(1, 3, 4, 0, 2, 5)
    return full.reshape(F, 2, 1024, 128), out.reshape(F, 2, 64, 128)


def solution(mesh):
    fine = Mesh(mesh.devices.reshape(2, 4, 2, 4, 2), SHOT + NODE)
    return jax.shard_map(
        shards,
        mesh=fine,
        in_specs=(P(None, SHOT, NODE), P(None, None, SHOT, NODE), P(), P(NODE)),
        out_specs=(P(None, None, None, NODE), P(None, None, SHOT, NODE)),
        check_vma=False,
    )
```

```python
import math

import jax
import jax.numpy as jnp
from jax import lax
from jax.experimental import pallas as pl
from jax.experimental.pallas import tpu as pltpu
from jax.sharding import Mesh, PartitionSpec as P

NODES = 1024
NT = 512
F = 4
SHOT = ("xl", "z", "core")
NODE = ("y", "xh")
PLANE = ("y", "xh", "xl", "core")
BF = jnp.bfloat16
F32 = jnp.float32
PARAMS = pltpu.CompilerParams(vmem_limit_bytes=40 * 1024 * 1024)


def local_table(freq_idx, first, count):
    sample = first + jnp.arange(count, dtype=jnp.int32)
    product = freq_idx[:, None] * sample[None, :] % NT
    angle = product.astype(F32) * (2.0 * math.pi / NT)
    stacked = jnp.stack([jnp.cos(angle), -jnp.sin(angle)], axis=1)
    return stacked.reshape(2 * F, count).astype(BF)


def struct(shape, dtype=F32):
    return jax.ShapeDtypeStruct(shape, dtype)


def cost(flops, moved):
    return pl.CostEstimate(flops=flops, bytes_accessed=moved, transcendentals=0)


def split(x):
    high = x.astype(BF)
    return high, (x - high.astype(F32)).astype(BF)


def stacked_split(x):
    return jnp.concatenate(split(x), axis=0)


def dot(a, b, transposed=False):
    dims = (((1,), (1 if transposed else 0,)), ((), ()))
    return lax.dot_general(a, b, dims, preferred_element_type=F32)


def product(both, field, transposed):
    high, low = split(field)
    first = dot(both, high, transposed)
    return first[:64] + first[64:] + dot(both[:64], low, transposed)


def lanes_sum(x):
    total = x[:, :128]
    for i in range(1, x.shape[1] // 128):
        total = total + x[:, i * 128 : (i + 1) * 128]
    return jnp.sum(total, axis=0, keepdims=True)


def total(rows):
    return jnp.sum(rows, axis=(0, 1), keepdims=True)


def transform_body(up_ref, table_ref, inverse_ref, out_ref, sums, exponents):
    block = (pl.program_id(0) * 2 + pl.program_id(1)) * 2 + pl.program_id(2)
    index = jnp.broadcast_to(inverse_ref[0:1, :], (64, 128))
    largest = jnp.zeros((64, 128), F32)
    for part in range(2):
        for group in range(8):
            x = up_ref[0, part, 0, group * 8 : group * 8 + 8].reshape(256, 128)
            y = dot(table_ref[...], x)
            y = jnp.take_along_axis(y, index, axis=1)
            largest = jnp.maximum(largest, jnp.abs(y))
            row = part * 64 + group * 8
            for fc in range(8):
                sums[fc, row : row + 8, :] = y[fc * 8 : fc * 8 + 8]
    peak = jnp.maximum(jnp.max(largest, axis=(0, 1), keepdims=True), 1e-30)
    exponent = jnp.floor(jnp.log(peak) * (1.0 / math.log(2.0))) - 14.0
    scale = jnp.exp2(-exponent)
    exponents[pl.ds(block, 1), :] = jnp.broadcast_to(exponent, (1, 128))
    rows = pl.multiple_of(block * 64, 64)
    for fc in range(8):
        scaled = jnp.floor(sums[fc].T * scale + 0.5)
        coded = jnp.clip(scaled, -32767.0, 32767.0).astype(jnp.int32).astype(jnp.int16)
        for k in range(4):
            dest = ((k // 2) * 4 + fc // 2) * 2 + k % 2
            out_ref[dest, pl.ds(rows + (fc % 2) * 32, 32), :] = coded[k * 32 : k * 32 + 32]

    @pl.when(block == 7)
    def _():
        tile = jnp.concatenate([exponents[...], jnp.zeros((8, 128), F32)], axis=0)
        coded = tile.astype(jnp.int32).astype(jnp.int16)
        for dest in range(16):
            out_ref[dest, 512:528, :] = coded


def transform(up_time, table, inverse):
    return pl.pallas_call(
        transform_body,
        grid=(2, 2, 2),
        in_specs=[
            pl.BlockSpec((1, 2, 1, 64, 32, 128), lambda x, c, z: (x, z, c, 0, 0, 0)),
            pl.BlockSpec((64, 256), lambda x, c, z: (0, 0)),
            pl.BlockSpec((8, 128), lambda x, c, z: (0, 0)),
        ],
        out_specs=pl.BlockSpec((16, 528, 128), lambda x, c, z: (0, 0, 0)),
        out_shape=struct((16, 528, 128), jnp.int16),
        scratch_shapes=[pltpu.VMEM((8, 128, 128), F32), pltpu.VMEM((8, 128), F32)],
        compiler_params=PARAMS,
        cost_estimate=cost(600_000_000, 10_000_000),
        name="transform",
    )(up_time.reshape(2, 4, 2, 64, 32, 128), table, inverse)


def collect_body(in_ref, out_ref):
    scales = [jnp.exp2(in_ref[i, 512:528, :].astype(F32)) for i in range(16)]
    for block in range(8):
        summed = jnp.zeros((64, 128), F32)
        for i in range(16):
            piece = in_ref[i, block * 64 : block * 64 + 64, :].astype(F32)
            summed = summed + piece * scales[i][block : block + 1]
        out_ref[:, block * 128 : block * 128 + 128] = summed


def collect(received):
    return pl.pallas_call(
        collect_body,
        out_shape=struct((64, 1024)),
        compiler_params=PARAMS,
        cost_estimate=cost(10_000_000, 3_000_000),
        name="collect",
    )(received)


def tile_of(down_ref, k, c):
    first = down_ref[0, k, :, c].reshape(256, 128)
    second = down_ref[1, k, :, c].reshape(256, 128)
    return jnp.concatenate([first, second], axis=1)


def adjoint_step(down_ref, both_ref):
    sums = [None, None]
    for k in range(4):
        both = both_ref[:, k * 256 : k * 256 + 256]
        for c in range(2):
            term = product(both, tile_of(down_ref, k, c), False)
            sums[c] = term if k == 0 else sums[c] + term
    real = sums[0][:32] + sums[1][32:]
    imaginary = sums[0][32:] - sums[1][:32]
    return jnp.concatenate([real, imaginary], axis=0)


def forward_step(down_ref, field, sums_ref, first):
    both = stacked_split(field)
    for c in range(2):
        for k in range(4):
            term = product(both, tile_of(down_ref, k, c), True)
            lanes = slice(k * 256, k * 256 + 256)

            @pl.when(first)
            def _():
                sums_ref[c, :, lanes] = term

            @pl.when(jnp.logical_not(first))
            def _():
                sums_ref[c, :, lanes] += term


def forward_end(sums_ref):
    real = sums_ref[0, :32] - sums_ref[1, 32:]
    imaginary = sums_ref[0, 32:] + sums_ref[1, :32]
    return jnp.concatenate([real, imaginary], axis=0)


def pack(field, out_ref, first):
    turned = field.T
    for k in range(8):
        piece = turned[k * 32 : k * 32 + 32]
        out_ref[first + k, 0:16, :] = jnp.concatenate([piece[:16], piece[16:]], axis=1)


def unpack(in_ref, first):
    pieces = [in_ref[first + k, 0:16, :] for k in range(4)]
    rows = []
    for c in range(2):
        for half in range(2):
            at = half * 64 + c * 32
            rows.append(jnp.concatenate([p[:, at : at + 32] for p in pieces], axis=1))
    return jnp.concatenate(rows, axis=0)


def symmetric(field, in_ref, first):
    mirrored = jnp.concatenate([unpack(in_ref, first), unpack(in_ref, first + 4)], axis=1)
    return (field + mirrored) * 0.5


DOWN_BLOCK = (2, 4, 4, 2, 64, 128)


def whole(shape):
    return pl.BlockSpec(shape, lambda *_: (0,) * len(shape))


def first_adjoint_body(data_ref, down_ref, field_ref, pieces_ref, both):
    @pl.when(pl.program_id(0) == 0)
    def _():
        both[...] = stacked_split(data_ref[...])

    field = adjoint_step(down_ref, both)
    field_ref[...] = field
    pack(field, pieces_ref, 0)


def first_adjoint(data, down):
    return pl.pallas_call(
        first_adjoint_body,
        grid=(4,),
        in_specs=[whole((64, 1024)), pl.BlockSpec(DOWN_BLOCK, lambda j: (j, 0, 0, 0, 0, 0))],
        out_specs=[
            pl.BlockSpec((64, 256), lambda j: (0, j)),
            pl.BlockSpec((8, 16, 128), lambda j: (j, 0, 0)),
        ],
        out_shape=[struct((64, 1024)), struct((32, 16, 128))],
        scratch_shapes=[pltpu.VMEM((128, 1024), BF)],
        compiler_params=PARAMS,
        cost_estimate=cost(800_000_000, 9_000_000),
        name="first_adjoint",
    )(data, down)


def second_body(
    field_ref, in_ref, down_ref, gradient_ref, image_ref, again_ref, out_ref, sums, both, norm
):
    phase, j = pl.program_id(0), pl.program_id(1)
    lanes = pl.ds(pl.multiple_of(j * 256, 256), 256)

    @pl.when(phase == 0)
    def _():
        gradient = symmetric(field_ref[:, lanes], in_ref, j * 8)
        gradient_ref[:, lanes] = gradient
        forward_step(down_ref, gradient, sums, j == 0)
        part = lanes_sum(gradient * gradient)
        norm[0:1, :] = jnp.where(j == 0, part, norm[0:1, :] + part)

    @pl.when((phase == 1) & (j == 0))
    def _():
        image = forward_end(sums)
        image_ref[...] = image
        both[...] = stacked_split(image)
        norm[1:2, :] = lanes_sum(image * image)

    @pl.when(phase == 1)
    def _():
        field = adjoint_step(down_ref, both)
        again_ref[:, lanes] = field
        pack(field, out_ref, j * 8)
        for k in range(8):
            out_ref[j * 8 + k, 16:24, :] = norm[...]


def second(field, received, down):
    return pl.pallas_call(
        second_body,
        grid=(2, 4),
        in_specs=[
            whole((64, 1024)),
            whole((32, 16, 128)),
            pl.BlockSpec(DOWN_BLOCK, lambda p, j: (j, 0, 0, 0, 0, 0)),
        ],
        out_specs=[whole((64, 1024))] * 3 + [whole((32, 24, 128))],
        out_shape=[struct((64, 1024))] * 3 + [struct((32, 24, 128))],
        scratch_shapes=[
            pltpu.VMEM((2, 64, 1024), F32),
            pltpu.VMEM((128, 1024), BF),
            pltpu.VMEM((8, 128), F32),
        ],
        compiler_params=PARAMS,
        cost_estimate=cost(1_600_000_000, 18_000_000),
        name="second",
    )(field, received, down)


def join_body(gradient_ref, again_ref, in_ref, out_ref):
    out_ref[0:64, :] = gradient_ref[...]
    for j in range(4):
        lanes = slice(j * 256, j * 256 + 256)
        out_ref[64:128, lanes] = symmetric(again_ref[:, lanes], in_ref, j * 8)


def join(gradient, again, received):
    return pl.pallas_call(
        join_body,
        out_shape=struct((128, 1024)),
        compiler_params=PARAMS,
        cost_estimate=cost(1_000_000, 2_000_000),
        name="join",
    )(gradient, again, received)


def first_step(in_ref):
    norm = total(jnp.sum(in_ref[:, 16:17, :], axis=0))
    curvature = total(jnp.sum(in_ref[:, 17:18, :], axis=0))
    return norm, curvature


def change_body(pair_ref, image_ref, in_ref, down_ref, change_ref, out_ref, sums):
    j = pl.program_id(0)
    lanes = pl.ds(pl.multiple_of(j * 256, 256), 256)
    forward_step(down_ref, pair_ref[64:128, lanes], sums, j == 0)

    @pl.when(j == 3)
    def _():
        norm, curvature = first_step(in_ref)
        step = norm / curvature
        image = image_ref[...]
        change = image - step * forward_end(sums)
        change_ref[...] = change
        gradient = pair_ref[0:64, :] - step * pair_ref[64:128, :]
        rows = jnp.concatenate(
            [
                lanes_sum(gradient * gradient),
                lanes_sum(change * change),
                lanes_sum(change * image),
                jnp.zeros((5, 128), F32),
            ],
            axis=0,
        )
        for i in range(32):
            out_ref[i] = rows


def changed(pair, image, received, down):
    return pl.pallas_call(
        change_body,
        grid=(4,),
        in_specs=[
            whole((128, 1024)),
            whole((64, 1024)),
            whole((32, 24, 128)),
            pl.BlockSpec(DOWN_BLOCK, lambda j: (j, 0, 0, 0, 0, 0)),
        ],
        out_specs=[whole((64, 1024)), whole((32, 8, 128))],
        out_shape=[struct((64, 1024)), struct((32, 8, 128))],
        scratch_shapes=[pltpu.VMEM((2, 64, 1024), F32)],
        compiler_params=PARAMS,
        cost_estimate=cost(800_000_000, 9_000_000),
        name="change",
    )(pair, image, received, down)


def residual_body(data_ref, image_ref, change_ref, in_ref, sums_ref, out_ref):
    norm, curvature = first_step(in_ref)
    step = norm / curvature
    rows = jnp.sum(sums_ref[...], axis=0)
    new_norm, change_change, change_image = (total(rows[i : i + 1]) for i in range(3))
    beta = new_norm / norm
    new_step = new_norm / (change_change + 2.0 * beta * change_image + beta * beta * curvature)
    image = image_ref[...]
    left = data_ref[...] - step * image - new_step * (change_ref[...] + beta * image)
    turned = left.T
    scalars = jnp.concatenate(
        [
            jnp.broadcast_to(step + new_step * (1.0 + beta), (1, 128)),
            jnp.broadcast_to(-new_step * step, (1, 128)),
            jnp.zeros((6, 128), F32),
        ],
        axis=0,
    )
    for dest in range(16):
        at = ((dest // 8) * 2 + dest % 2) * 256 + (dest // 2 % 4) * 64
        piece = turned[at : at + 64]
        out_ref[dest, 0:32, :] = jnp.concatenate([piece[:32], piece[32:]], axis=1)
        out_ref[dest, 32:40, :] = scalars


def residual_of(data, image, change, received, sums):
    return pl.pallas_call(
        residual_body,
        out_shape=struct((16, 40, 128)),
        compiler_params=PARAMS,
        cost_estimate=cost(2_000_000, 2_000_000),
        name="residual",
    )(data, image, change, received, sums)


def place_body(in_ref, out_ref):
    for f in range(F):
        pieces = [in_ref[(k // 2 * 4 + f) * 2 + k % 2, 0:32, :] for k in range(4)]
        for c in range(2):
            for half in range(2):
                at = half * 64 + c * 32
                row = jnp.concatenate([p[:, at : at + 32] for p in pieces], axis=1)
                out_ref[f, c, half * 32 : half * 32 + 32, :] = row


def place(received):
    return pl.pallas_call(
        place_body,
        out_shape=struct((F, 2, 64, 128)),
        compiler_params=PARAMS,
        cost_estimate=cost(1_000_000, 1_000_000),
        name="place",
    )(received)


def combine_body(pairs_ref, scalars_ref, out_ref):
    first = scalars_ref[0, 0, 0, 0:1, :]
    second_ = scalars_ref[0, 0, 0, 1:2, :]
    for j in range(8):
        lanes = slice(j * 128, j * 128 + 128)
        rows = [
            pairs_ref[k // 2, 0, k % 2, 0, 0, :, lanes] * first
            + pairs_ref[k // 2, 0, k % 2, 1, 0, :, lanes] * second_
            for k in range(4)
        ]
        out_ref[0, 0, lanes, :] = jnp.concatenate(rows, axis=0).T


def combine(pairs, received):
    return pl.pallas_call(
        combine_body,
        grid=(F, 2),
        in_specs=[
            pl.BlockSpec((2, 1, 2, 2, 1, 32, 1024), lambda f, c: (0, f, 0, 0, c, 0, 0)),
            pl.BlockSpec((1, 1, 1, 8, 128), lambda f, c: (0, f, 0, 4, 0)),
        ],
        out_specs=pl.BlockSpec((1, 1, 1024, 128), lambda f, c: (f, c, 0, 0)),
        out_shape=struct((F, 2, 1024, 128)),
        compiler_params=PARAMS,
        cost_estimate=cost(10_000_000, 12_000_000),
        name="combine",
    )(pairs.reshape(2, F, 2, 2, 2, 32, 1024), received.reshape(2, F, 2, 40, 128))


def shards(up_time, downgoing, freq_idx, node_map):
    own = lax.all_to_all(downgoing, "z", 0, 0, tiled=True)
    down = lax.all_gather(own.reshape(512, 128), PLANE, axis=0, tiled=True)
    down = down.reshape(8, 4, 4, 2, 64, 128)

    count = up_time.shape[1]
    table = local_table(freq_idx, lax.axis_index(SHOT) * count, count)
    table = table[:, None, None, :] * jnp.eye(8, dtype=BF)[None, :, :, None]
    slots = jnp.arange(128, dtype=jnp.int32)
    inverse = jnp.sum(jnp.where(node_map[:, None] == slots[None, :], slots[:, None], 0), axis=0)
    inverse = jnp.broadcast_to(inverse[None, :], (8, 128))
    pieces = transform(up_time, table.reshape(64, 256), inverse)
    data = collect(lax.all_to_all(pieces, SHOT, 0, 0, tiled=True))

    field, pieces = first_adjoint(data, down)
    received = lax.all_to_all(pieces, PLANE, 0, 0, tiled=True)
    gradient, image, again, pieces = second(field, received, down)
    received = lax.all_to_all(pieces, PLANE, 0, 0, tiled=True)
    pair = join(gradient, again, received)
    pairs = lax.all_gather(pair, SHOT, axis=0, tiled=True)
    change, sums = changed(pair, image, received, down)
    sums = lax.all_to_all(sums, PLANE, 0, 0, tiled=True)
    left = lax.all_to_all(residual_of(data, image, change, received, sums), SHOT, 0, 0, tiled=True)
    return combine(pairs, left), place(left)


def solution(mesh):
    fine = Mesh(mesh.devices.reshape(2, 4, 2, 4, 2), SHOT + NODE)
    return jax.shard_map(
        shards,
        mesh=fine,
        in_specs=(P(None, SHOT, NODE), P(None, None, SHOT, NODE), P(), P(NODE)),
        out_specs=(P(None, None, None, NODE), P(None, None, SHOT, NODE)),
        check_vma=False,
    )
```

```python
import math

import jax
import jax.numpy as jnp
from jax import lax
from jax.experimental import pallas as pl
from jax.experimental.pallas import tpu as pltpu
from jax.sharding import Mesh, PartitionSpec as P

NODES = 1024
NT = 512
F = 4
SHOT = ("xl", "z", "core")
NODE = ("y", "xh")
CHIPS = ("xl", "z")
PLANE_CHIPS = ("y", "xh", "xl")
PLANE = ("y", "xh", "xl", "core")
BF = jnp.bfloat16
F32 = jnp.float32
SMALL = pltpu.CompilerParams(vmem_limit_bytes=16 * 1024 * 1024)
LARGE = pltpu.CompilerParams(vmem_limit_bytes=32 * 1024 * 1024)
FULL = pltpu.CompilerParams(vmem_limit_bytes=58 * 1024 * 1024)


def local_table(freq_idx, first, count):
    sample = first + jnp.arange(count, dtype=jnp.int32)
    product = freq_idx[:, None] * sample[None, :] % NT
    angle = product.astype(F32) * (2.0 * math.pi / NT)
    stacked = jnp.stack([jnp.cos(angle), -jnp.sin(angle)], axis=1)
    return stacked.reshape(2 * F, count).astype(BF)


def struct(shape, dtype=F32):
    return jax.ShapeDtypeStruct(shape, dtype)


def cost(flops, moved):
    return pl.CostEstimate(flops=flops, bytes_accessed=moved, transcendentals=0)


def split(x):
    high = x.astype(BF)
    return high, (x - high.astype(F32)).astype(BF)


def stacked_split(x):
    return jnp.concatenate(split(x), axis=0)


def dot(a, b):
    return lax.dot_general(a, b, (((1,), (0,)), ((), ())), preferred_element_type=F32)


def whole(shape):
    return pl.BlockSpec(shape, lambda *_: (0,) * len(shape))


def exponent_of(peak):
    return jnp.floor(jnp.log(jnp.maximum(peak, 1e-30)) * (1.0 / math.log(2.0))) - 14.0


def code(x):
    return jnp.clip(jnp.floor(x + 0.5), -32767.0, 32767.0).astype(jnp.int32).astype(jnp.int16)


def peak_of(x):
    return jnp.max(jnp.abs(x), axis=(0, 1), keepdims=True)


def exponent_tile(rows, lanes):
    rows = [jnp.broadcast_to(r, (1, lanes)) for r in rows]
    rows.append(jnp.zeros((16 - len(rows), lanes), F32))
    return jnp.concatenate(rows, axis=0).astype(jnp.int32).astype(jnp.int16)


def lanes_sum(x):
    total = x[:, :128]
    for i in range(1, x.shape[1] // 128):
        total = total + x[:, i * 128 : (i + 1) * 128]
    return jnp.sum(total, axis=0, keepdims=True)


def total(rows):
    return jnp.sum(rows, axis=(0, 1), keepdims=True)


def transform_body(
    up_ref, table_ref, inverse_ref, mine_ref, other_ref, sums, exponents, held, arrived
):
    block = pl.program_id(0)
    me = lax.axis_index("core")

    def fetch(i):
        source = up_ref.at[i // 4, pl.ds(i % 2 * 2, 2), i // 2 % 2]
        return pltpu.make_async_copy(source, held.at[i], arrived.at[i])

    @pl.when(block == 0)
    def _():
        for i in range(8):
            fetch(i).start()

    fetch(block).wait()
    index = jnp.broadcast_to(inverse_ref[0:1, :], (64, 128))
    largest = jnp.zeros((64, 128), F32)
    for part in range(2):
        for group in range(4):
            row = group * 16
            x = [held[block, part, row + h * 8 : row + h * 8 + 8].reshape(256, 128) for h in range(2)]
            both = dot(table_ref[...], jnp.concatenate(x, axis=1))
            for h in range(2):
                y = jnp.take_along_axis(both[:, h * 128 : h * 128 + 128], index, axis=1)
                largest = jnp.maximum(largest, jnp.abs(y))
                at = part * 64 + row + h * 8
                for fc in range(8):
                    sums[fc, at : at + 8, :] = y[fc * 8 : fc * 8 + 8]
    exponent = exponent_of(peak_of(largest))
    scale = jnp.exp2(-exponent)
    exponents[pl.ds(block, 1), :] = jnp.broadcast_to(exponent, (1, 128))
    rows = pl.multiple_of(block * 64, 64)
    for fc in range(8):
        turned = sums[fc].T * scale
        at = pl.ds(rows + (fc % 2) * 32, 32)
        for x in range(2):
            first, second_ = (turned[x * 64 + c * 32 : x * 64 + c * 32 + 32] for c in range(2))
            mine_ref[x * 4 + fc // 2, at, :] = code(jnp.where(me == 0, first, second_))
            other_ref[x * 4 + fc // 2, at, :] = code(jnp.where(me == 0, second_, first))

    @pl.when(block == 7)
    def _():
        coded = exponent_tile([exponents[i : i + 1, :] for i in range(8)], 128)
        for dest in range(8):
            mine_ref[dest, 512:528, :] = coded
            other_ref[dest, 512:528, :] = coded


def transform(up_time, table, inverse):
    return pl.pallas_call(
        transform_body,
        grid=(8,),
        in_specs=[
            pl.BlockSpec(memory_space=pl.ANY),
            whole((64, 256)),
            whole((8, 128)),
        ],
        out_specs=[whole((8, 528, 128))] * 2,
        out_shape=[struct((8, 528, 128), jnp.int16)] * 2,
        scratch_shapes=[
            pltpu.VMEM((8, 128, 128), F32),
            pltpu.VMEM((8, 128), F32),
            pltpu.VMEM((8, 2, 64, 32, 128), BF),
            pltpu.SemaphoreType.DMA((8,)),
        ],
        compiler_params=FULL,
        cost_estimate=cost(600_000_000, 10_000_000),
        name="transform",
    )(up_time.reshape(2, 4, 2, 64, 32, 128), table, inverse)


def merge_body(mine_ref, other_ref, out_ref):
    scales = [jnp.exp2(r[0, 512:528, :].astype(F32)) for r in (mine_ref, other_ref)]
    exponents = []
    for block in range(8):
        rows = slice(block * 64, block * 64 + 64)
        sums, largest = [], jnp.zeros((64, 128), F32)
        for dest in range(8):
            mine = mine_ref[dest, rows, :].astype(F32) * scales[0][block : block + 1]
            sums.append(mine + other_ref[dest, rows, :].astype(F32) * scales[1][block : block + 1])
            largest = jnp.maximum(largest, jnp.abs(sums[-1]))
        exponents.append(exponent_of(peak_of(largest)))
        scale = jnp.exp2(-exponents[-1])
        for dest in range(8):
            out_ref[dest, rows, :] = code(sums[dest] * scale)
    coded = exponent_tile(exponents, 128)
    for dest in range(8):
        out_ref[dest, 512:528, :] = coded


def merge(pieces, other):
    return pl.pallas_call(
        merge_body,
        out_shape=struct((8, 528, 128), jnp.int16),
        compiler_params=SMALL,
        cost_estimate=cost(10_000_000, 3_000_000),
        name="merge",
    )(pieces, other)


def collect_body(in_ref, out_ref):
    scales = [jnp.exp2(in_ref[i, 512:528, :].astype(F32)) for i in range(8)]
    for block in range(8):
        summed = jnp.zeros((64, 128), F32)
        for i in range(8):
            piece = in_ref[i, block * 64 : block * 64 + 64, :].astype(F32)
            summed = summed + piece * scales[i][block : block + 1]
        out_ref[:, block * 128 : block * 128 + 128] = summed


def collect(received):
    return pl.pallas_call(
        collect_body,
        out_shape=struct((64, 1024)),
        compiler_params=SMALL,
        cost_estimate=cost(5_000_000, 2_000_000),
        name="collect",
    )(received)


def code_down_body(in_ref, out_ref):
    for f in range(F):
        field = in_ref[f].reshape(128, 128)
        exponent = exponent_of(peak_of(field))
        out_ref[f, 0:128, :] = code(field * jnp.exp2(-exponent))
        out_ref[f, 128:144, :] = exponent_tile([exponent], 128)


def code_down(downgoing):
    return pl.pallas_call(
        code_down_body,
        out_shape=struct((F, 144, 128), jnp.int16),
        compiler_params=SMALL,
        cost_estimate=cost(1_000_000, 500_000),
        name="code_down",
    )(downgoing)


def adjoint_step(down_ref, both):
    sums = []
    for c in range(2):
        first = dot(both, down_ref[0, c])
        sums.append(first[:64] + first[64:] + dot(both[:64], down_ref[1, c]))
    real = sums[0][:32] + sums[1][32:]
    imaginary = sums[0][32:] - sums[1][:32]
    return jnp.concatenate([real, imaginary], axis=0)


def forward_step(down_ref, both):
    sums = []
    for c in range(2):
        first = dot(down_ref[0, c], both) + dot(down_ref[1, c], both)
        sums.append((first[:, :64] + first[:, 64:]).T)
    real = sums[0][:32] - sums[1][32:]
    imaginary = sums[0][32:] + sums[1][:32]
    return jnp.concatenate([real, imaginary], axis=0)


def side_split(field):
    return jnp.concatenate(split(field.T), axis=1)


def pack(field, out_ref, first):
    turned = field.T
    for k in range(8):
        piece = turned[k * 32 : k * 32 + 32]
        out_ref[first + k, 0:16, :] = jnp.concatenate([piece[:16], piece[16:]], axis=1)


def unpack(in_ref, first):
    pieces = [in_ref[first + k, 0:16, :] for k in range(4)]
    rows = []
    for c in range(2):
        for half in range(2):
            at = half * 64 + c * 32
            rows.append(jnp.concatenate([p[:, at : at + 32] for p in pieces], axis=1))
    return jnp.concatenate(rows, axis=0)


def symmetric(field, in_ref, first):
    mirrored = jnp.concatenate([unpack(in_ref, first), unpack(in_ref, first + 4)], axis=1)
    return (field + mirrored) * 0.5


BY_NODES = (2, 2, 1024, 256)
BY_SHOTS = (2, 2, 256, 1024)


def decode_body(mine_ref, other_ref, down_ref):
    me = lax.axis_index("core")
    for source, core in ((mine_ref, me), (other_ref, 1 - me)):
        for n in range(2):
            for x in range(2):
                for z in range(4):
                    scale = jnp.exp2(source[n, x, z, 128:144, :].astype(F32))[0:1]
                    first = x * 512 + core * 256 + z * 64
                    rows = pl.ds(pl.multiple_of(first, 64), 64)
                    for c in range(2):
                        field = source[n, x, z, c * 64 : c * 64 + 64, :].astype(F32) * scale
                        high, low = split(field)
                        down_ref[0, c, rows, n * 128 : n * 128 + 128] = high
                        down_ref[1, c, rows, n * 128 : n * 128 + 128] = low


def decode(mine, other):
    block = pl.BlockSpec((2, 2, 4, 144, 128), lambda j: (j, 0, 0, 0, 0))
    return pl.pallas_call(
        decode_body,
        grid=(4,),
        in_specs=[block, block],
        out_specs=pl.BlockSpec(BY_NODES, lambda j: (0, 0, 0, j)),
        out_shape=struct((2, 2, 1024, 1024), BF),
        compiler_params=LARGE,
        cost_estimate=cost(20_000_000, 13_000_000),
        name="decode",
    )(mine.reshape(8, 2, 4, 144, 128), other.reshape(8, 2, 4, 144, 128))


def first_adjoint_body(data_ref, by_nodes_ref, field_ref, pieces_ref, both):
    @pl.when(pl.program_id(0) == 0)
    def _():
        both[...] = stacked_split(data_ref[...])

    field = adjoint_step(by_nodes_ref, both[...])
    field_ref[...] = field
    pack(field, pieces_ref, 0)


def first_adjoint(data, down):
    return pl.pallas_call(
        first_adjoint_body,
        grid=(4,),
        in_specs=[whole((64, 1024)), pl.BlockSpec(BY_NODES, lambda j: (0, 0, 0, j))],
        out_specs=[
            pl.BlockSpec((64, 256), lambda j: (0, j)),
            pl.BlockSpec((8, 16, 128), lambda j: (j, 0, 0)),
        ],
        out_shape=[struct((64, 1024)), struct((32, 16, 128))],
        scratch_shapes=[pltpu.VMEM((128, 1024), BF)],
        compiler_params=LARGE,
        cost_estimate=cost(800_000_000, 9_000_000),
        name="first_adjoint",
    )(data, down)


def second_body(
    field_ref, in_ref, by_shots_ref, by_nodes_ref, gradient_ref, image_ref, again_ref, out_ref,
    side, both, norm,
):
    phase, j = pl.program_id(0), pl.program_id(1)
    lanes = pl.ds(pl.multiple_of(j * 256, 256), 256)

    @pl.when((phase == 0) & (j == 0))
    def _():
        for i in range(4):
            at = slice(i * 256, i * 256 + 256)
            gradient = symmetric(field_ref[:, at], in_ref, i * 8)
            gradient_ref[:, at] = gradient
            side[at, :] = side_split(gradient)
        gradient = gradient_ref[...]
        norm[...] = jnp.zeros((8, 128), F32)
        norm[0:1, :] = lanes_sum(gradient * gradient)

    @pl.when(phase == 0)
    def _():
        image = forward_step(by_shots_ref, side[...])
        image_ref[:, lanes] = image
        both[:, lanes] = stacked_split(image)
        norm[1:2, :] += lanes_sum(image * image)

    @pl.when(phase == 1)
    def _():
        field = adjoint_step(by_nodes_ref, both[...])
        again_ref[:, lanes] = field
        pack(field, out_ref, j * 8)
        for k in range(8):
            out_ref[j * 8 + k, 16:24, :] = norm[...]


def second(field, received, down):
    return pl.pallas_call(
        second_body,
        grid=(2, 4),
        in_specs=[
            whole((64, 1024)),
            whole((32, 16, 128)),
            pl.BlockSpec(BY_SHOTS, lambda p, j: (0, 0, jnp.where(p == 0, j, 3), 0)),
            pl.BlockSpec(BY_NODES, lambda p, j: (0, 0, 0, jnp.where(p == 0, 0, j))),
        ],
        out_specs=[whole((64, 1024))] * 3 + [whole((32, 24, 128))],
        out_shape=[struct((64, 1024))] * 3 + [struct((32, 24, 128))],
        scratch_shapes=[
            pltpu.VMEM((1024, 128), BF),
            pltpu.VMEM((128, 1024), BF),
            pltpu.VMEM((8, 128), F32),
        ],
        compiler_params=LARGE,
        cost_estimate=cost(1_600_000_000, 18_000_000),
        name="second",
    )(field, received, down, down)


def first_step(in_ref):
    norm = total(jnp.sum(in_ref[:, 16:17, :], axis=0))
    curvature = total(jnp.sum(in_ref[:, 17:18, :], axis=0))
    return norm, curvature


def change_body(
    gradient_ref, field_ref, image_ref, in_ref, by_shots_ref, again_ref, change_ref, out_ref, side, sums
):
    j = pl.program_id(0)
    lanes = pl.ds(pl.multiple_of(j * 256, 256), 256)
    norm, curvature = first_step(in_ref)
    step = norm / curvature

    @pl.when(j == 0)
    def _():
        for i in range(4):
            at = slice(i * 256, i * 256 + 256)
            again = symmetric(field_ref[:, at], in_ref, i * 8)
            again_ref[:, at] = again
            side[at, :] = side_split(again)
        sums[...] = jnp.zeros((8, 128), F32)
        gradient = gradient_ref[...] - step * again_ref[...]
        sums[0:1, :] = lanes_sum(gradient * gradient)

    image = image_ref[:, lanes]
    change = image - step * forward_step(by_shots_ref, side[...])
    change_ref[:, lanes] = change
    sums[1:2, :] += lanes_sum(change * change)
    sums[2:3, :] += lanes_sum(change * image)

    @pl.when(j == 3)
    def _():
        for i in range(32):
            out_ref[i] = sums[...]


def changed(gradient, field, image, received, down):
    return pl.pallas_call(
        change_body,
        grid=(4,),
        in_specs=[
            whole((64, 1024)),
            whole((64, 1024)),
            whole((64, 1024)),
            whole((32, 24, 128)),
            pl.BlockSpec(BY_SHOTS, lambda j: (0, 0, j, 0)),
        ],
        out_specs=[whole((64, 1024)), whole((64, 1024)), whole((32, 8, 128))],
        out_shape=[struct((64, 1024)), struct((64, 1024)), struct((32, 8, 128))],
        scratch_shapes=[pltpu.VMEM((1024, 128), BF), pltpu.VMEM((8, 128), F32)],
        compiler_params=LARGE,
        cost_estimate=cost(800_000_000, 9_000_000),
        name="change",
    )(gradient, field, image, received, down)


def update_body(
    data_ref, gradient_ref, again_ref, image_ref, change_ref, in_ref, sums_ref, out_ref
):
    norm, curvature = first_step(in_ref)
    step = norm / curvature
    rows = jnp.sum(sums_ref[...], axis=0)
    new_norm, change_change, change_image = (total(rows[i : i + 1]) for i in range(3))
    beta = new_norm / norm
    new_step = new_norm / (change_change + 2.0 * beta * change_image + beta * beta * curvature)
    gradient, image = gradient_ref[...], image_ref[...]
    direction = (gradient - step * again_ref[...]) + beta * gradient
    result = step * gradient + new_step * direction
    left = data_ref[...] - step * image - new_step * (change_ref[...] + beta * image)
    exponents = [exponent_of(peak_of(result)), exponent_of(peak_of(left))]
    coded = code(result * jnp.exp2(-exponents[0]))
    turned = (left * jnp.exp2(-exponents[1])).T
    tile = exponent_tile(exponents, 128)
    for dest in range(8):
        for j in range(8):
            out_ref[dest, j * 64 : j * 64 + 64, :] = coded[:, j * 128 : j * 128 + 128]
        for core in range(2):
            at = (dest // 4 * 2 + core) * 256 + dest % 4 * 64
            piece = jnp.concatenate([turned[at : at + 32], turned[at + 32 : at + 64]], axis=1)
            out_ref[dest, 512 + core * 32 : 544 + core * 32, :] = code(piece)
        out_ref[dest, 576:592, :] = tile


def updated(data, gradient, again, image, change, received, sums):
    return pl.pallas_call(
        update_body,
        out_shape=struct((8, 592, 128), jnp.int16),
        compiler_params=SMALL,
        cost_estimate=cost(5_000_000, 3_000_000),
        name="update",
    )(data, gradient, again, image, change, received, sums)


def finish_body(mine_ref, other_ref, reflectivity_ref, residual_ref, held, arrived):
    f = pl.program_id(0)
    me = lax.axis_index("core")

    def fetch(i, x, k):
        source = (mine_ref, other_ref)[k].at[x, i]
        slot = me if k == 0 else 1 - me
        return pltpu.make_async_copy(source, held.at[i, x, slot], arrived.at[i, x, k])

    @pl.when(f == 0)
    def _():
        for i in range(F):
            for x in range(2):
                for k in range(2):
                    fetch(i, x, k).start()

    for x in range(2):
        for k in range(2):
            fetch(f, x, k).wait()

    scales = []
    for k in range(4):
        scales.append(jnp.exp2(held[f, k // 2, k % 2, 576:592, :].astype(F32)))
    for c in range(2):
        for j in range(8):
            at = slice(j * 64 + c * 32, j * 64 + c * 32 + 32)
            parts = [held[f, k // 2, k % 2, at, :].astype(F32) * scales[k][0:1] for k in range(4)]
            whole_rows = jnp.concatenate(parts, axis=0)
            reflectivity_ref[0, c, j * 128 : j * 128 + 128, :] = whole_rows.T
    first = pl.multiple_of(512 + me * 32, 32)
    pieces = [
        held[f, k // 2, k % 2, pl.ds(first, 32), :].astype(F32) * scales[k][1:2] for k in range(4)
    ]
    for c in range(2):
        for half in range(2):
            at = half * 64 + c * 32
            row = jnp.concatenate([p[:, at : at + 32] for p in pieces], axis=1)
            residual_ref[0, c, half * 32 : half * 32 + 32, :] = row


def finish(mine, other):
    return pl.pallas_call(
        finish_body,
        grid=(F,),
        in_specs=[pl.BlockSpec(memory_space=pl.ANY)] * 2,
        out_specs=[
            pl.BlockSpec((1, 2, 1024, 128), lambda f: (f, 0, 0, 0)),
            pl.BlockSpec((1, 2, 64, 128), lambda f: (f, 0, 0, 0)),
        ],
        out_shape=[struct((F, 2, 1024, 128)), struct((F, 2, 64, 128))],
        scratch_shapes=[
            pltpu.VMEM((F, 2, 2, 592, 128), jnp.int16),
            pltpu.SemaphoreType.DMA((F, 2, 2)),
        ],
        compiler_params=LARGE,
        cost_estimate=cost(10_000_000, 7_000_000),
        name="finish",
    )(mine.reshape(2, F, 592, 128), other.reshape(2, F, 592, 128))


def swap_cores(x):
    return lax.ppermute(x, "core", [(0, 1), (1, 0)])


def shards(up_time, downgoing, freq_idx, node_map):
    own = lax.all_to_all(code_down(downgoing), "z", 0, 0, tiled=True)
    mine = lax.all_gather(own.reshape(576, 128), PLANE_CHIPS, axis=0, tiled=True)
    down = decode(mine, swap_cores(mine))

    count = up_time.shape[1]
    table = local_table(freq_idx, lax.axis_index(SHOT) * count, count)
    table = table[:, None, None, :] * jnp.eye(8, dtype=BF)[None, :, :, None]
    slots = jnp.arange(128, dtype=jnp.int32)
    inverse = jnp.sum(jnp.where(node_map[:, None] == slots[None, :], slots[:, None], 0), axis=0)
    inverse = jnp.broadcast_to(inverse[None, :], (8, 128))
    pieces, others = transform(up_time, table.reshape(64, 256), inverse)
    pieces = merge(pieces, swap_cores(others))
    data = collect(lax.all_to_all(pieces, CHIPS, 0, 0, tiled=True))

    field, pieces = first_adjoint(data, down)
    received = lax.all_to_all(pieces, PLANE, 0, 0, tiled=True)
    gradient, image, field, pieces = second(field, received, down)
    received = lax.all_to_all(pieces, PLANE, 0, 0, tiled=True)
    again, change, sums = changed(gradient, field, image, received, down)
    sums = lax.all_to_all(sums, PLANE, 0, 0, tiled=True)
    pieces = updated(data, gradient, again, image, change, received, sums)
    mine = lax.all_to_all(pieces, CHIPS, 0, 0, tiled=True)
    return tuple(finish(mine, swap_cores(mine)))


def solution(mesh):
    fine = Mesh(mesh.devices.reshape(2, 4, 2, 4, 2), SHOT + NODE)
    return jax.shard_map(
        shards,
        mesh=fine,
        in_specs=(P(None, SHOT, NODE), P(None, None, SHOT, NODE), P(), P(NODE)),
        out_specs=(P(None, None, None, NODE), P(None, None, SHOT, NODE)),
        check_vma=False,
    )
```

```python
import math

import jax
import jax.numpy as jnp
from jax import lax
from jax.experimental import pallas as pl
from jax.experimental.pallas import tpu as pltpu
from jax.sharding import Mesh, PartitionSpec as P

NODES = 1024
NT = 512
F = 4
SHOT = ("xl", "z", "core")
NODE = ("y", "xh")
CHIPS = ("xl", "z")
PLANE_CHIPS = ("y", "xh", "xl")
PLANE = ("y", "xh", "xl", "core")
BF = jnp.bfloat16
F32 = jnp.float32
SMALL = pltpu.CompilerParams(vmem_limit_bytes=16 * 1024 * 1024)
FULL = pltpu.CompilerParams(vmem_limit_bytes=58 * 1024 * 1024)


def local_table(freq_idx, first, count):
    sample = first + jnp.arange(count, dtype=jnp.int32)
    product = freq_idx[:, None] * sample[None, :] % NT
    angle = product.astype(F32) * (2.0 * math.pi / NT)
    stacked = jnp.stack([jnp.cos(angle), -jnp.sin(angle)], axis=1)
    return stacked.reshape(2 * F, count).astype(BF)


def struct(shape, dtype=F32):
    return jax.ShapeDtypeStruct(shape, dtype)


def cost(flops, moved):
    return pl.CostEstimate(flops=flops, bytes_accessed=moved, transcendentals=0)


def split(x):
    high = x.astype(BF)
    return high, (x - high.astype(F32)).astype(BF)


def stacked_split(x):
    return jnp.concatenate(split(x), axis=0)


def dot(a, b):
    return lax.dot_general(a, b, (((1,), (0,)), ((), ())), preferred_element_type=F32)


def whole(shape):
    return pl.BlockSpec(shape, lambda *_: (0,) * len(shape))


def exponent_of(peak):
    return jnp.floor(jnp.log(jnp.maximum(peak, 1e-30)) * (1.0 / math.log(2.0))) - 14.0


def code(x):
    return jnp.clip(jnp.floor(x + 0.5), -32767.0, 32767.0).astype(jnp.int32).astype(jnp.int16)


def peak_of(x):
    return jnp.max(jnp.abs(x), axis=(0, 1), keepdims=True)


def exponent_tile(rows, lanes):
    rows = [jnp.broadcast_to(r, (1, lanes)) for r in rows]
    rows.append(jnp.zeros((16 - len(rows), lanes), F32))
    return jnp.concatenate(rows, axis=0).astype(jnp.int32).astype(jnp.int16)


def lanes_sum(x):
    total = x[:, :128]
    for i in range(1, x.shape[1] // 128):
        total = total + x[:, i * 128 : (i + 1) * 128]
    return jnp.sum(total, axis=0, keepdims=True)


def total(rows):
    return jnp.sum(rows, axis=(0, 1), keepdims=True)


def transform_body(
    up_ref, table_ref, inverse_ref, mine_ref, other_ref, sums, exponents, held, arrived
):
    block = pl.program_id(0)
    me = lax.axis_index("core")

    def fetch(i):
        source = up_ref.at[i // 4, pl.ds(i % 2 * 2, 2), i // 2 % 2]
        return pltpu.make_async_copy(source, held.at[i], arrived.at[i])

    @pl.when(block == 0)
    def _():
        for i in range(8):
            fetch(i).start()

    fetch(block).wait()
    index = jnp.broadcast_to(inverse_ref[0:1, :], (64, 128))
    largest = jnp.zeros((64, 128), F32)
    for part in range(2):
        for group in range(4):
            row = group * 16
            x = [held[block, part, row + h * 8 : row + h * 8 + 8].reshape(256, 128) for h in range(2)]
            both = dot(table_ref[...], jnp.concatenate(x, axis=1))
            for h in range(2):
                y = jnp.take_along_axis(both[:, h * 128 : h * 128 + 128], index, axis=1)
                largest = jnp.maximum(largest, jnp.abs(y))
                at = part * 64 + row + h * 8
                for fc in range(8):
                    sums[fc, at : at + 8, :] = y[fc * 8 : fc * 8 + 8]
    exponent = exponent_of(peak_of(largest))
    scale = jnp.exp2(-exponent)
    exponents[pl.ds(block, 1), :] = jnp.broadcast_to(exponent, (1, 128))
    rows = pl.multiple_of(block * 64, 64)
    for fc in range(8):
        turned = sums[fc].T * scale
        at = pl.ds(rows + (fc % 2) * 32, 32)
        for x in range(2):
            first, second_ = (turned[x * 64 + c * 32 : x * 64 + c * 32 + 32] for c in range(2))
            mine_ref[x * 4 + fc // 2, at, :] = code(jnp.where(me == 0, first, second_))
            other_ref[x * 4 + fc // 2, at, :] = code(jnp.where(me == 0, second_, first))

    @pl.when(block == 7)
    def _():
        coded = exponent_tile([exponents[i : i + 1, :] for i in range(8)], 128)
        for dest in range(8):
            mine_ref[dest, 512:528, :] = coded
            other_ref[dest, 512:528, :] = coded


def transform(up_time, table, inverse):
    return pl.pallas_call(
        transform_body,
        grid=(8,),
        in_specs=[
            pl.BlockSpec(memory_space=pl.ANY),
            whole((64, 256)),
            whole((8, 128)),
        ],
        out_specs=[whole((8, 528, 128))] * 2,
        out_shape=[struct((8, 528, 128), jnp.int16)] * 2,
        scratch_shapes=[
            pltpu.VMEM((8, 128, 128), F32),
            pltpu.VMEM((8, 128), F32),
            pltpu.VMEM((8, 2, 64, 32, 128), BF),
            pltpu.SemaphoreType.DMA((8,)),
        ],
        compiler_params=FULL,
        cost_estimate=cost(600_000_000, 10_000_000),
        name="transform",
    )(up_time.reshape(2, 4, 2, 64, 32, 128), table, inverse)


def merge_body(mine_ref, other_ref, out_ref):
    scales = [jnp.exp2(r[0, 512:528, :].astype(F32)) for r in (mine_ref, other_ref)]
    exponents = []
    for block in range(8):
        rows = slice(block * 64, block * 64 + 64)
        sums, largest = [], jnp.zeros((64, 128), F32)
        for dest in range(8):
            mine = mine_ref[dest, rows, :].astype(F32) * scales[0][block : block + 1]
            sums.append(mine + other_ref[dest, rows, :].astype(F32) * scales[1][block : block + 1])
            largest = jnp.maximum(largest, jnp.abs(sums[-1]))
        exponents.append(exponent_of(peak_of(largest)))
        scale = jnp.exp2(-exponents[-1])
        for dest in range(8):
            out_ref[dest, rows, :] = code(sums[dest] * scale)
    coded = exponent_tile(exponents, 128)
    for dest in range(8):
        out_ref[dest, 512:528, :] = coded


def merge(pieces, other):
    return pl.pallas_call(
        merge_body,
        out_shape=struct((8, 528, 128), jnp.int16),
        compiler_params=SMALL,
        cost_estimate=cost(10_000_000, 3_000_000),
        name="merge",
    )(pieces, other)


def collect_body(in_ref, out_ref):
    scales = [jnp.exp2(in_ref[i, 512:528, :].astype(F32)) for i in range(8)]
    for block in range(8):
        summed = jnp.zeros((64, 128), F32)
        for i in range(8):
            piece = in_ref[i, block * 64 : block * 64 + 64, :].astype(F32)
            summed = summed + piece * scales[i][block : block + 1]
        out_ref[:, block * 128 : block * 128 + 128] = summed


def collect(received):
    return pl.pallas_call(
        collect_body,
        out_shape=struct((64, 1024)),
        compiler_params=SMALL,
        cost_estimate=cost(5_000_000, 2_000_000),
        name="collect",
    )(received)


def code_down_body(in_ref, out_ref):
    for f in range(F):
        field = in_ref[f].reshape(128, 128)
        exponent = exponent_of(peak_of(field))
        coded = code(field * jnp.exp2(-exponent))
        tile = exponent_tile([exponent], 128)
        for i in range(16):
            out_ref[f * 16 + i, 0:128, :] = coded
            out_ref[f * 16 + i, 128:144, :] = tile


def code_down(downgoing):
    return pl.pallas_call(
        code_down_body,
        out_shape=struct((64, 144, 128), jnp.int16),
        compiler_params=FULL,
        cost_estimate=cost(1_000_000, 3_000_000),
        name="code_down",
    )(downgoing)


def adjoint_step(down_ref, both, nodes=slice(None)):
    sums = []
    for c in range(2):
        first = dot(both, down_ref[0, c, :, nodes])
        sums.append(first[:64] + first[64:] + dot(both[:64], down_ref[1, c, :, nodes]))
    real = sums[0][:32] + sums[1][32:]
    imaginary = sums[0][32:] - sums[1][:32]
    return jnp.concatenate([real, imaginary], axis=0)


def forward_step(down_ref, both, shots):
    sums = []
    for c in range(2):
        first = dot(down_ref[0, c, shots, :], both) + dot(down_ref[1, c, shots, :], both)
        sums.append((first[:, :64] + first[:, 64:]).T)
    real = sums[0][:32] - sums[1][32:]
    imaginary = sums[0][32:] + sums[1][:32]
    return jnp.concatenate([real, imaginary], axis=0)


def side_split(field):
    return jnp.concatenate(split(field.T), axis=1)


def pack(field, out_ref, first):
    turned = field.T
    for k in range(8):
        piece = turned[k * 32 : k * 32 + 32]
        out_ref[first + k, 0:16, :] = jnp.concatenate([piece[:16], piece[16:]], axis=1)


def unpack(in_ref, first):
    pieces = [in_ref[first + k, 0:16, :] for k in range(4)]
    rows = []
    for c in range(2):
        for half in range(2):
            at = half * 64 + c * 32
            rows.append(jnp.concatenate([p[:, at : at + 32] for p in pieces], axis=1))
    return jnp.concatenate(rows, axis=0)


def symmetric(field, in_ref, first):
    mirrored = jnp.concatenate([unpack(in_ref, first), unpack(in_ref, first + 4)], axis=1)
    return (field + mirrored) * 0.5


HELD = pl.BlockSpec(memory_space=pltpu.VMEM)


def decode_body(mine_ref, other_ref, down_ref):
    me = lax.axis_index("core")
    for n in range(8):
        lanes = slice(n * 128, n * 128 + 128)
        for source, core in ((mine_ref, me), (other_ref, 1 - me)):
            for x in range(2):
                for z in range(4):
                    scale = jnp.exp2(source[z, n, x, 128:144, :].astype(F32))[0:1]
                    first = x * 512 + core * 256 + z * 64
                    rows = pl.ds(pl.multiple_of(first, 64), 64)
                    for c in range(2):
                        field = source[z, n, x, c * 64 : c * 64 + 64, :].astype(F32) * scale
                        high, low = split(field)
                        down_ref[0, c, rows, lanes] = high
                        down_ref[1, c, rows, lanes] = low


def decode(mine, other):
    return pl.pallas_call(
        decode_body,
        in_specs=[HELD] * 2,
        out_specs=HELD,
        out_shape=struct((2, 2, 1024, 1024), BF),
        compiler_params=SMALL,
        cost_estimate=cost(20_000_000, 13_000_000),
        name="decode",
    )(mine.reshape(4, 8, 2, 144, 128), other.reshape(4, 8, 2, 144, 128))


def first_adjoint_body(data_ref, down_ref, field_ref, pieces_ref):
    both = stacked_split(data_ref[...])
    for i in range(4):
        at = slice(i * 256, i * 256 + 256)
        field = adjoint_step(down_ref, both, at)
        field_ref[:, at] = field
        pack(field, pieces_ref, i * 8)


def first_adjoint(data, down):
    return pl.pallas_call(
        first_adjoint_body,
        in_specs=[HELD] * 2,
        out_specs=[HELD] * 2,
        out_shape=[struct((64, 1024)), struct((32, 16, 128))],
        compiler_params=SMALL,
        cost_estimate=cost(800_000_000, 9_000_000),
        name="first_adjoint",
    )(data, down)


def second_body(field_ref, in_ref, down_ref, gradient_ref, image_ref, again_ref, out_ref, side, both):
    blocks = [slice(i * 256, i * 256 + 256) for i in range(4)]
    for i, at in enumerate(blocks):
        gradient = symmetric(field_ref[:, at], in_ref, i * 8)
        gradient_ref[:, at] = gradient
        side[at, :] = side_split(gradient)
    for at in blocks:
        image = forward_step(down_ref, side[...], at)
        image_ref[:, at] = image
        both[:, at] = stacked_split(image)
    gradient, image = gradient_ref[...], image_ref[...]
    rows = [lanes_sum(gradient * gradient), lanes_sum(image * image), jnp.zeros((6, 128), F32)]
    norm = jnp.concatenate(rows, axis=0)
    for i, at in enumerate(blocks):
        field = adjoint_step(down_ref, both[...], at)
        again_ref[:, at] = field
        pack(field, out_ref, i * 8)
    for k in range(32):
        out_ref[k, 16:24, :] = norm


def second(field, received, down):
    return pl.pallas_call(
        second_body,
        in_specs=[HELD] * 3,
        out_specs=[HELD] * 4,
        out_shape=[struct((64, 1024))] * 3 + [struct((32, 24, 128))],
        scratch_shapes=[pltpu.VMEM((1024, 128), BF), pltpu.VMEM((128, 1024), BF)],
        compiler_params=SMALL,
        cost_estimate=cost(1_600_000_000, 18_000_000),
        name="second",
    )(field, received, down)


def first_step(in_ref):
    norm = total(jnp.sum(in_ref[:, 16:17, :], axis=0))
    curvature = total(jnp.sum(in_ref[:, 17:18, :], axis=0))
    return norm, curvature


def change_body(
    gradient_ref, field_ref, image_ref, in_ref, down_ref, again_ref, change_ref, out_ref, side
):
    blocks = [slice(i * 256, i * 256 + 256) for i in range(4)]
    norm, curvature = first_step(in_ref)
    step = norm / curvature
    for i, at in enumerate(blocks):
        again = symmetric(field_ref[:, at], in_ref, i * 8)
        again_ref[:, at] = again
        side[at, :] = side_split(again)
    for at in blocks:
        change_ref[:, at] = image_ref[:, at] - step * forward_step(down_ref, side[...], at)
    gradient = gradient_ref[...] - step * again_ref[...]
    change = change_ref[...]
    rows = [gradient * gradient, change * change, change * image_ref[...]]
    rows = [lanes_sum(row) for row in rows] + [jnp.zeros((5, 128), F32)]
    sums = jnp.concatenate(rows, axis=0)
    for i in range(32):
        out_ref[i] = sums


def changed(gradient, field, image, received, down):
    return pl.pallas_call(
        change_body,
        in_specs=[HELD] * 5,
        out_specs=[HELD] * 3,
        out_shape=[struct((64, 1024)), struct((64, 1024)), struct((32, 8, 128))],
        scratch_shapes=[pltpu.VMEM((1024, 128), BF)],
        compiler_params=SMALL,
        cost_estimate=cost(800_000_000, 9_000_000),
        name="change",
    )(gradient, field, image, received, down)


def side_by_side(field):
    turned = field.T
    return jnp.concatenate([turned[:512], turned[512:]], axis=1)


def update_body(
    data_ref, gradient_ref, again_ref, image_ref, change_ref, in_ref, sums_ref, out_ref
):
    norm, curvature = first_step(in_ref)
    step = norm / curvature
    rows = jnp.sum(sums_ref[...], axis=0)
    new_norm, change_change, change_image = (total(rows[i : i + 1]) for i in range(3))
    beta = new_norm / norm
    new_step = new_norm / (change_change + 2.0 * beta * change_image + beta * beta * curvature)
    gradient, image = gradient_ref[...], image_ref[...]
    direction = (gradient - step * again_ref[...]) + beta * gradient
    result = step * gradient + new_step * direction
    left = data_ref[...] - step * image - new_step * (change_ref[...] + beta * image)
    exponents = [exponent_of(peak_of(result)), exponent_of(peak_of(left))]
    own = lax.axis_index("xl") * 2 + lax.axis_index("core")
    coded = code(pltpu.roll(side_by_side(result * jnp.exp2(-exponents[0])), own * 32, 1))
    turned = (left * jnp.exp2(-exponents[1])).T
    tile = exponent_tile(exponents, 128)
    for dest in range(8):
        out_ref[dest, 0:512, :] = coded
        for core in range(2):
            at = (dest // 4 * 2 + core) * 256 + dest % 4 * 64
            piece = jnp.concatenate([turned[at : at + 32], turned[at + 32 : at + 64]], axis=1)
            out_ref[dest, 512 + core * 32 : 544 + core * 32, :] = code(piece)
        out_ref[dest, 576:592, :] = tile


def updated(data, gradient, again, image, change, received, sums):
    return pl.pallas_call(
        update_body,
        out_shape=struct((8, 592, 128), jnp.int16),
        compiler_params=SMALL,
        cost_estimate=cost(5_000_000, 3_000_000),
        name="update",
    )(data, gradient, again, image, change, received, sums)


def place(f, first_ref, second_ref, core, reflectivity_ref, residual_ref):
    refs = [ref.at[x, f] for x in range(2) for ref in (first_ref, second_ref)]
    scales = [jnp.exp2(ref[576:592, :].astype(F32)) for ref in refs]
    owner = lax.broadcasted_iota(jnp.int32, (64, 128), 1) // 32
    spread = scales[3][0:1]
    for k in range(3):
        spread = jnp.where(owner[0:1] == k, scales[k][0:1], spread)
    for j in range(8):
        parts = [ref[j * 64 : j * 64 + 64, :].astype(F32) for ref in refs]
        for q in range(4):
            mixed = parts[(3 - q) % 4]
            for b in range(3):
                mixed = jnp.where(owner == b, parts[(b - q) % 4], mixed)
            if q:
                mixed = pltpu.roll(mixed, 128 - 32 * q, 1)
            first = q // 2 * 512 + j * 64
            reflectivity_ref[0, q % 2, first : first + 64, :] = mixed * spread
    rows = slice(512 + core * 32, 544 + core * 32)
    pieces = [ref[rows, :].astype(F32) * scale[1:2] for ref, scale in zip(refs, scales)]
    for c in range(2):
        for half in range(2):
            at = half * 64 + c * 32
            row = jnp.concatenate([p[:, at : at + 32] for p in pieces], axis=1)
            residual_ref[0, c, half * 32 : half * 32 + 32, :] = row


def finish_body(mine_ref, other_ref, reflectivity_ref, residual_ref):
    f = pl.program_id(0)
    me = lax.axis_index("core")

    @pl.when(me == 0)
    def _():
        place(f, mine_ref, other_ref, 0, reflectivity_ref, residual_ref)

    @pl.when(me == 1)
    def _():
        place(f, other_ref, mine_ref, 1, reflectivity_ref, residual_ref)


def finish(mine, other):
    return pl.pallas_call(
        finish_body,
        grid=(F,),
        in_specs=[HELD] * 2,
        out_specs=[
            pl.BlockSpec((1, 2, 1024, 128), lambda f: (f, 0, 0, 0)),
            pl.BlockSpec((1, 2, 64, 128), lambda f: (f, 0, 0, 0)),
        ],
        out_shape=[struct((F, 2, 1024, 128)), struct((F, 2, 64, 128))],
        compiler_params=SMALL,
        cost_estimate=cost(10_000_000, 7_000_000),
        name="finish",
    )(mine.reshape(2, F, 592, 128), other.reshape(2, F, 592, 128))


def swap_cores(x):
    return lax.ppermute(x, "core", [(0, 1), (1, 0)])


def shards(up_time, downgoing, freq_idx, node_map):
    mine = lax.all_to_all(code_down(downgoing), ("z",) + PLANE_CHIPS, 0, 0, tiled=True)
    count = up_time.shape[1]
    table = local_table(freq_idx, lax.axis_index(SHOT) * count, count)
    table = table[:, None, None, :] * jnp.eye(8, dtype=BF)[None, :, :, None]
    slots = jnp.arange(128, dtype=jnp.int32)
    inverse = jnp.sum(jnp.where(node_map[:, None] == slots[None, :], slots[:, None], 0), axis=0)
    inverse = jnp.broadcast_to(inverse[None, :], (8, 128))
    pieces, others = transform(up_time, table.reshape(64, 256), inverse)
    pieces = merge(pieces, swap_cores(others))
    mine, pieces = lax.optimization_barrier((mine, pieces))
    down = decode(mine, swap_cores(mine))
    received = lax.all_to_all(pieces, CHIPS, 0, 0, tiled=True)
    data = collect(received)

    field, pieces = first_adjoint(data, down)
    received = lax.all_to_all(pieces, PLANE, 0, 0, tiled=True)
    gradient, image, field, pieces = second(field, received, down)
    received = lax.all_to_all(pieces, PLANE, 0, 0, tiled=True)
    again, change, sums = changed(gradient, field, image, received, down)
    sums = lax.all_to_all(sums, PLANE, 0, 0, tiled=True)
    pieces = updated(data, gradient, again, image, change, received, sums)
    mine = lax.all_to_all(pieces, CHIPS, 0, 0, tiled=True)
    return tuple(finish(mine, swap_cores(mine)))


def solution(mesh):
    fine = Mesh(mesh.devices.reshape(2, 4, 2, 4, 2), SHOT + NODE)
    return jax.shard_map(
        shards,
        mesh=fine,
        in_specs=(P(None, SHOT, NODE), P(None, None, SHOT, NODE), P(), P(NODE)),
        out_specs=(P(None, None, None, NODE), P(None, None, SHOT, NODE)),
        check_vma=False,
    )
```

```python
import math

import jax
import jax.numpy as jnp
from jax import lax
from jax.experimental import pallas as pl
from jax.experimental.pallas import tpu as pltpu
from jax.sharding import Mesh, PartitionSpec as P

NODES = 1024
NT = 512
F = 4
SHOT = ("xl", "z", "core")
NODE = ("y", "xh")
CHIPS = ("xl", "z")
ORDER = (6, 7, 5, 2, 3, 1, 4)
PLANE_CHIPS = ("y", "xh", "xl")
PLANE = ("y", "xh", "xl", "core")
BF = jnp.bfloat16
F32 = jnp.float32
HELD = pl.BlockSpec(memory_space=pltpu.VMEM)
SMALL = pltpu.CompilerParams(vmem_limit_bytes=16 * 1024 * 1024)
FULL = pltpu.CompilerParams(vmem_limit_bytes=58 * 1024 * 1024)


def local_table(freq_idx, first, count):
    sample = first + jnp.arange(count, dtype=jnp.int32)
    product = freq_idx[:, None] * sample[None, :] % NT
    angle = product.astype(F32) * (2.0 * math.pi / NT)
    stacked = jnp.stack([jnp.cos(angle), -jnp.sin(angle)], axis=1)
    return stacked.reshape(2 * F, count).astype(BF)


def struct(shape, dtype=F32):
    return jax.ShapeDtypeStruct(shape, dtype)


def cost(flops, moved):
    return pl.CostEstimate(flops=flops, bytes_accessed=moved, transcendentals=0)


def split(x):
    high = x.astype(BF)
    return high, (x - high.astype(F32)).astype(BF)


def stacked_split(x):
    return jnp.concatenate(split(x), axis=0)


def dot(a, b):
    return lax.dot_general(a, b, (((1,), (0,)), ((), ())), preferred_element_type=F32)


def whole(shape):
    return pl.BlockSpec(shape, lambda *_: (0,) * len(shape))


def exponent_of(peak):
    return jnp.floor(jnp.log(jnp.maximum(peak, 1e-30)) * (1.0 / math.log(2.0))) - 14.0


def code(x):
    return jnp.clip(jnp.floor(x + 0.5), -32767.0, 32767.0).astype(jnp.int32).astype(jnp.int16)


def peak_of(x):
    return jnp.max(jnp.abs(x), axis=(0, 1), keepdims=True)


def exponent_tile(rows, lanes):
    rows = [jnp.broadcast_to(r, (1, lanes)) for r in rows]
    rows.append(jnp.zeros((16 - len(rows), lanes), F32))
    return jnp.concatenate(rows, axis=0).astype(jnp.int32).astype(jnp.int16)


def lanes_sum(x):
    total = x[:, :128]
    for i in range(1, x.shape[1] // 128):
        total = total + x[:, i * 128 : (i + 1) * 128]
    return jnp.sum(total, axis=0, keepdims=True)


def total(rows):
    return jnp.sum(rows, axis=(0, 1), keepdims=True)


def transform_body(up_ref, table_ref, inverse_ref, mine_ref, other_ref, sums, exponents):
    me = lax.axis_index("core")
    index = jnp.broadcast_to(inverse_ref[...], (64, 128))
    table = jnp.concatenate([table_ref[...].astype(F32)] * 8, axis=1)
    table = jnp.broadcast_to(table[:, None, :], (8, 8, 256)).reshape(64, 256)
    shot = lax.broadcasted_iota(jnp.int32, (64, 256), 0) % 8
    table = jnp.where(shot == lax.broadcasted_iota(jnp.int32, (64, 256), 1) // 32, table, 0.0).astype(BF)

    def step(block, carry):
        chip, core, first = block // 4, block // 2 % 2, block % 2 * 2
        largest = jnp.zeros((64, 128), F32)
        for pair in range(8):
            part, row = first + pair // 4, pair % 4 * 16
            x = [up_ref[chip, part, core, row + h * 8 : row + h * 8 + 8].reshape(256, 128) for h in range(2)]
            both = dot(table, jnp.concatenate(x, axis=1))
            for h in range(2):
                y = jnp.take_along_axis(both[:, h * 128 : h * 128 + 128], index, axis=1)
                largest = jnp.maximum(largest, jnp.abs(y))
                at = pair // 4 * 64 + row + h * 8
                for fc in range(8):
                    sums[fc, at : at + 8, :] = y[fc * 8 : fc * 8 + 8]
        exponent = exponent_of(peak_of(largest))
        scale = jnp.exp2(-exponent)
        exponents[pl.ds(block, 1), :] = jnp.broadcast_to(exponent, (1, 128))
        rows = pl.multiple_of(block * 64, 64)
        for fc in range(8):
            turned = sums[fc].T * scale
            at = pl.ds(rows + (fc % 2) * 32, 32)
            for x in range(2):
                lower, upper = (turned[x * 64 + c * 32 : x * 64 + c * 32 + 32] for c in range(2))
                mine_ref[x * 4 + fc // 2, at, :] = code(jnp.where(me == 0, lower, upper))
                other_ref[x * 4 + fc // 2, at, :] = code(jnp.where(me == 0, upper, lower))
        return carry

    lax.fori_loop(0, 8, step, 0)
    coded = exponent_tile([exponents[i : i + 1, :] for i in range(8)], 128)
    for dest in range(8):
        mine_ref[dest, 512:528, :] = coded
        other_ref[dest, 512:528, :] = coded


def transform(up_time, table, inverse):
    return pl.pallas_call(
        transform_body,
        in_specs=[HELD] * 3,
        out_specs=[HELD] * 2,
        out_shape=[struct((8, 528, 128), jnp.int16)] * 2,
        scratch_shapes=[pltpu.VMEM((8, 128, 128), F32), pltpu.VMEM((8, 128), F32)],
        compiler_params=SMALL,
        cost_estimate=cost(600_000_000, 10_000_000),
        name="transform",
    )(up_time.reshape(2, 4, 2, 64, 32, 128), table, inverse)


def merge_body(mine_ref, other_ref, *out_refs):
    chip = lax.axis_index("xl") * 4 + lax.axis_index("z")
    scales = [jnp.exp2(r[0, 512:528, :].astype(F32)) for r in (mine_ref, other_ref)]
    exponents = []
    for block in range(8):
        rows = slice(block * 64, block * 64 + 64)
        sums, largest = [], jnp.zeros((64, 128), F32)
        for i in range(8):
            dest = chip ^ i
            mine = mine_ref[dest, rows, :].astype(F32) * scales[0][block : block + 1]
            sums.append(mine + other_ref[dest, rows, :].astype(F32) * scales[1][block : block + 1])
            largest = jnp.maximum(largest, jnp.abs(sums[-1]))
        exponents.append(exponent_of(peak_of(largest)))
        scale = jnp.exp2(-exponents[-1])
        for i in range(8):
            out_refs[i][rows, :] = code(sums[i] * scale)
    coded = exponent_tile(exponents, 128)
    for out_ref in out_refs:
        out_ref[512:528, :] = coded


def merge(pieces, other):
    return pl.pallas_call(
        merge_body,
        out_shape=[struct((528, 128), jnp.int16)] * 8,
        compiler_params=SMALL,
        cost_estimate=cost(10_000_000, 3_000_000),
        name="merge",
    )(pieces, other)


def collect_body(*refs):
    in_refs, out_ref = refs[:-1], refs[-1]
    scales = [jnp.exp2(ref[512:528, :].astype(F32)) for ref in in_refs]
    for block in range(8):
        summed = jnp.zeros((64, 128), F32)
        for ref, scale in zip(in_refs, scales):
            piece = ref[block * 64 : block * 64 + 64, :].astype(F32)
            summed = summed + piece * scale[block : block + 1]
        out_ref[:, block * 128 : block * 128 + 128] = summed


def collect(received):
    return pl.pallas_call(
        collect_body,
        out_shape=struct((64, 1024)),
        compiler_params=SMALL,
        cost_estimate=cost(5_000_000, 2_000_000),
        name="collect",
    )(*received)


def code_down_body(in_ref, out_ref):
    for f in range(F):
        field = in_ref[f].reshape(128, 128)
        exponent = exponent_of(peak_of(field))
        coded = code(field * jnp.exp2(-exponent))
        tile = exponent_tile([exponent], 128)
        for i in range(16):
            out_ref[f * 16 + i, 0:128, :] = coded
            out_ref[f * 16 + i, 128:144, :] = tile


def code_down(downgoing):
    return pl.pallas_call(
        code_down_body,
        out_shape=struct((64, 144, 128), jnp.int16),
        compiler_params=FULL,
        cost_estimate=cost(1_000_000, 3_000_000),
        name="code_down",
    )(downgoing)


def adjoint_step(down_ref, both, nodes=slice(None)):
    sums = []
    for c in range(2):
        first = dot(both, down_ref[0, c, :, nodes])
        sums.append(first[:64] + first[64:] + dot(both[:64], down_ref[1, c, :, nodes]))
    real = sums[0][:32] + sums[1][32:]
    imaginary = sums[0][32:] - sums[1][:32]
    return jnp.concatenate([real, imaginary], axis=0)


def forward_step(down_ref, both, shots):
    sums = []
    for c in range(2):
        first = dot(down_ref[0, c, shots, :], both) + dot(down_ref[1, c, shots, :], both)
        sums.append((first[:, :64] + first[:, 64:]).T)
    real = sums[0][:32] - sums[1][32:]
    imaginary = sums[0][32:] + sums[1][:32]
    return jnp.concatenate([real, imaginary], axis=0)


def side_split(field):
    return jnp.concatenate(split(field.T), axis=1)


def pack(field, out_ref, first):
    turned = field.T
    for k in range(8):
        piece = turned[k * 32 : k * 32 + 32]
        out_ref[first + k, 0:16, :] = jnp.concatenate([piece[:16], piece[16:]], axis=1)


def unpack(in_ref, first):
    pieces = [in_ref[first + k, 0:16, :] for k in range(4)]
    rows = []
    for c in range(2):
        for half in range(2):
            at = half * 64 + c * 32
            rows.append(jnp.concatenate([p[:, at : at + 32] for p in pieces], axis=1))
    return jnp.concatenate(rows, axis=0)


def symmetric(field, in_ref, first):
    mirrored = jnp.concatenate([unpack(in_ref, first), unpack(in_ref, first + 4)], axis=1)
    return (field + mirrored) * 0.5


def decode_body(mine_ref, other_ref, down_ref):
    me = lax.axis_index("core")
    for n in range(8):
        lanes = slice(n * 128, n * 128 + 128)
        for source, core in ((mine_ref, me), (other_ref, 1 - me)):
            for x in range(2):
                for z in range(4):
                    scale = jnp.exp2(source[z, n, x, 128:144, :].astype(F32))[0:1]
                    first = x * 512 + core * 256 + z * 64
                    rows = pl.ds(pl.multiple_of(first, 64), 64)
                    for c in range(2):
                        field = source[z, n, x, c * 64 : c * 64 + 64, :].astype(F32) * scale
                        high, low = split(field)
                        down_ref[0, c, rows, lanes] = high
                        down_ref[1, c, rows, lanes] = low


def decode(mine, other):
    return pl.pallas_call(
        decode_body,
        in_specs=[HELD] * 2,
        out_specs=HELD,
        out_shape=struct((2, 2, 1024, 1024), BF),
        compiler_params=SMALL,
        cost_estimate=cost(20_000_000, 13_000_000),
        name="decode",
    )(mine.reshape(4, 8, 2, 144, 128), other.reshape(4, 8, 2, 144, 128))


def first_adjoint_body(data_ref, down_ref, field_ref, pieces_ref):
    both = stacked_split(data_ref[...])
    for i in range(4):
        at = slice(i * 256, i * 256 + 256)
        field = adjoint_step(down_ref, both, at)
        field_ref[:, at] = field
        pack(field, pieces_ref, i * 8)


def first_adjoint(data, down):
    return pl.pallas_call(
        first_adjoint_body,
        in_specs=[HELD] * 2,
        out_specs=[HELD] * 2,
        out_shape=[struct((64, 1024)), struct((32, 16, 128))],
        compiler_params=SMALL,
        cost_estimate=cost(800_000_000, 9_000_000),
        name="first_adjoint",
    )(data, down)


def second_body(field_ref, in_ref, down_ref, gradient_ref, image_ref, again_ref, out_ref, side, both):
    blocks = [slice(i * 256, i * 256 + 256) for i in range(4)]
    for i, at in enumerate(blocks):
        gradient = symmetric(field_ref[:, at], in_ref, i * 8)
        gradient_ref[:, at] = gradient
        side[at, :] = side_split(gradient)
    for at in blocks:
        image = forward_step(down_ref, side[...], at)
        image_ref[:, at] = image
        both[:, at] = stacked_split(image)
    gradient, image = gradient_ref[...], image_ref[...]
    rows = [lanes_sum(gradient * gradient), lanes_sum(image * image), jnp.zeros((6, 128), F32)]
    norm = jnp.concatenate(rows, axis=0)
    for i, at in enumerate(blocks):
        field = adjoint_step(down_ref, both[...], at)
        again_ref[:, at] = field
        pack(field, out_ref, i * 8)
    for k in range(32):
        out_ref[k, 16:24, :] = norm


def second(field, received, down):
    return pl.pallas_call(
        second_body,
        in_specs=[HELD] * 3,
        out_specs=[HELD] * 4,
        out_shape=[struct((64, 1024))] * 3 + [struct((32, 24, 128))],
        scratch_shapes=[pltpu.VMEM((1024, 128), BF), pltpu.VMEM((128, 1024), BF)],
        compiler_params=SMALL,
        cost_estimate=cost(1_600_000_000, 18_000_000),
        name="second",
    )(field, received, down)


def first_step(in_ref):
    norm = total(jnp.sum(in_ref[:, 16:17, :], axis=0))
    curvature = total(jnp.sum(in_ref[:, 17:18, :], axis=0))
    return norm, curvature


def change_body(
    gradient_ref, field_ref, image_ref, in_ref, down_ref, again_ref, change_ref, out_ref, side
):
    blocks = [slice(i * 256, i * 256 + 256) for i in range(4)]
    norm, curvature = first_step(in_ref)
    step = norm / curvature
    for i, at in enumerate(blocks):
        again = symmetric(field_ref[:, at], in_ref, i * 8)
        again_ref[:, at] = again
        side[at, :] = side_split(again)
    for at in blocks:
        change_ref[:, at] = image_ref[:, at] - step * forward_step(down_ref, side[...], at)
    gradient = gradient_ref[...] - step * again_ref[...]
    change = change_ref[...]
    rows = [gradient * gradient, change * change, change * image_ref[...]]
    rows = [lanes_sum(row) for row in rows] + [jnp.zeros((5, 128), F32)]
    sums = jnp.concatenate(rows, axis=0)
    for i in range(32):
        out_ref[i] = sums


def changed(gradient, field, image, received, down):
    return pl.pallas_call(
        change_body,
        in_specs=[HELD] * 5,
        out_specs=[HELD] * 3,
        out_shape=[struct((64, 1024)), struct((64, 1024)), struct((32, 8, 128))],
        scratch_shapes=[pltpu.VMEM((1024, 128), BF)],
        compiler_params=SMALL,
        cost_estimate=cost(800_000_000, 9_000_000),
        name="change",
    )(gradient, field, image, received, down)


def side_by_side(field):
    turned = field.T
    return jnp.concatenate([turned[:512], turned[512:]], axis=1)


def update_body(
    data_ref, gradient_ref, again_ref, image_ref, change_ref, in_ref, sums_ref, out_ref
):
    norm, curvature = first_step(in_ref)
    step = norm / curvature
    rows = jnp.sum(sums_ref[...], axis=0)
    new_norm, change_change, change_image = (total(rows[i : i + 1]) for i in range(3))
    beta = new_norm / norm
    new_step = new_norm / (change_change + 2.0 * beta * change_image + beta * beta * curvature)
    gradient, image = gradient_ref[...], image_ref[...]
    direction = (gradient - step * again_ref[...]) + beta * gradient
    result = step * gradient + new_step * direction
    left = data_ref[...] - step * image - new_step * (change_ref[...] + beta * image)
    exponents = [exponent_of(peak_of(result)), exponent_of(peak_of(left))]
    own = lax.axis_index("xl") * 2 + lax.axis_index("core")
    coded = code(pltpu.roll(side_by_side(result * jnp.exp2(-exponents[0])), own * 32, 1))
    turned = (left * jnp.exp2(-exponents[1])).T
    tile = exponent_tile(exponents, 128)
    for dest in range(8):
        out_ref[dest, 0:512, :] = coded
        for core in range(2):
            at = (dest // 4 * 2 + core) * 256 + dest % 4 * 64
            piece = jnp.concatenate([turned[at : at + 32], turned[at + 32 : at + 64]], axis=1)
            out_ref[dest, 512 + core * 32 : 544 + core * 32, :] = code(piece)
        out_ref[dest, 576:592, :] = tile


def updated(data, gradient, again, image, change, received, sums):
    return pl.pallas_call(
        update_body,
        out_shape=struct((8, 592, 128), jnp.int16),
        compiler_params=SMALL,
        cost_estimate=cost(5_000_000, 3_000_000),
        name="update",
    )(data, gradient, again, image, change, received, sums)


def place(f, first_ref, second_ref, core, reflectivity_ref, residual_ref):
    refs = [ref.at[x, f] for x in range(2) for ref in (first_ref, second_ref)]
    scales = [jnp.exp2(ref[576:592, :].astype(F32)) for ref in refs]
    owner = lax.broadcasted_iota(jnp.int32, (64, 128), 1) // 32
    spread = scales[3][0:1]
    for k in range(3):
        spread = jnp.where(owner[0:1] == k, scales[k][0:1], spread)
    for j in range(8):
        parts = [ref[j * 64 : j * 64 + 64, :].astype(F32) for ref in refs]
        for q in range(4):
            mixed = parts[(3 - q) % 4]
            for b in range(3):
                mixed = jnp.where(owner == b, parts[(b - q) % 4], mixed)
            if q:
                mixed = pltpu.roll(mixed, 128 - 32 * q, 1)
            first = q // 2 * 512 + j * 64
            reflectivity_ref[0, q % 2, first : first + 64, :] = mixed * spread
    rows = slice(512 + core * 32, 544 + core * 32)
    pieces = [ref[rows, :].astype(F32) * scale[1:2] for ref, scale in zip(refs, scales)]
    for c in range(2):
        for half in range(2):
            at = half * 64 + c * 32
            row = jnp.concatenate([p[:, at : at + 32] for p in pieces], axis=1)
            residual_ref[0, c, half * 32 : half * 32 + 32, :] = row


def finish_body(mine_ref, other_ref, reflectivity_ref, residual_ref):
    f = pl.program_id(0)
    me = lax.axis_index("core")

    @pl.when(me == 0)
    def _():
        place(f, mine_ref, other_ref, 0, reflectivity_ref, residual_ref)

    @pl.when(me == 1)
    def _():
        place(f, other_ref, mine_ref, 1, reflectivity_ref, residual_ref)


def finish(mine, other):
    return pl.pallas_call(
        finish_body,
        grid=(F,),
        in_specs=[HELD] * 2,
        out_specs=[
            pl.BlockSpec((1, 2, 1024, 128), lambda f: (f, 0, 0, 0)),
            pl.BlockSpec((1, 2, 64, 128), lambda f: (f, 0, 0, 0)),
        ],
        out_shape=[struct((F, 2, 1024, 128)), struct((F, 2, 64, 128))],
        compiler_params=SMALL,
        cost_estimate=cost(10_000_000, 7_000_000),
        name="finish",
    )(mine.reshape(2, F, 592, 128), other.reshape(2, F, 592, 128))


def swap_cores(x):
    return lax.ppermute(x, "core", [(0, 1), (1, 0)])


def shards(up_time, downgoing, freq_idx, node_map):
    mine = lax.all_to_all(code_down(downgoing), ("z",) + PLANE_CHIPS, 0, 0, tiled=True)
    count = up_time.shape[1]
    table = local_table(freq_idx, lax.axis_index(SHOT) * count, count)
    slots = jnp.arange(128, dtype=jnp.int32)
    inverse = jnp.sum(jnp.where(node_map[:, None] == slots[None, :], slots[:, None], 0), axis=0)
    pieces, others = transform(up_time, table, inverse[None, :])
    pieces = merge(pieces, swap_cores(others))
    received = [lax.ppermute(pieces[i], CHIPS, [(k, k ^ i) for k in range(8)]) for i in ORDER]
    mine, received[:4] = lax.optimization_barrier((mine, received[:4]))
    down = decode(mine, swap_cores(mine))
    received[4:], down = lax.optimization_barrier((received[4:], down))
    data = collect([pieces[0], *received])

    field, pieces = first_adjoint(data, down)
    received = lax.all_to_all(pieces, PLANE, 0, 0, tiled=True)
    gradient, image, field, pieces = second(field, received, down)
    received = lax.all_to_all(pieces, PLANE, 0, 0, tiled=True)
    again, change, sums = changed(gradient, field, image, received, down)
    sums = lax.all_to_all(sums, PLANE, 0, 0, tiled=True)
    pieces = updated(data, gradient, again, image, change, received, sums)
    mine = lax.all_to_all(pieces, CHIPS, 0, 0, tiled=True)
    return tuple(finish(mine, swap_cores(mine)))


def solution(mesh):
    fine = Mesh(mesh.devices.reshape(2, 4, 2, 4, 2), SHOT + NODE)
    return jax.shard_map(
        shards,
        mesh=fine,
        in_specs=(P(None, SHOT, NODE), P(None, None, SHOT, NODE), P(), P(NODE)),
        out_specs=(P(None, None, None, NODE), P(None, None, SHOT, NODE)),
        check_vma=False,
    )
```

```python
import math

import jax
import jax.numpy as jnp
from jax import lax
from jax.experimental import pallas as pl
from jax.experimental.pallas import tpu as pltpu
from jax.sharding import Mesh, PartitionSpec as P

NODES = 1024
NT = 512
F = 4
SHOT = ("xl", "z", "core")
NODE = ("y", "xh")
CHIPS = ("xl", "z")
ORDER = (6, 7, 5, 2, 3, 1, 4)
ALL_CHIPS = ("xl", "xh", "y", "z")
PLANE = ("y", "xh", "xl", "core")
BF = jnp.bfloat16
F32 = jnp.float32
HELD = pl.BlockSpec(memory_space=pltpu.VMEM)
SMALL = pltpu.CompilerParams(vmem_limit_bytes=16 * 1024 * 1024)
FULL = pltpu.CompilerParams(vmem_limit_bytes=58 * 1024 * 1024)


def local_table(freq_idx, first, count):
    sample = first + jnp.arange(count, dtype=jnp.int32)
    product = freq_idx[:, None] * sample[None, :] % NT
    angle = product.astype(F32) * (2.0 * math.pi / NT)
    stacked = jnp.stack([jnp.cos(angle), -jnp.sin(angle)], axis=1)
    return stacked.reshape(2 * F, count).astype(BF)


def struct(shape, dtype=F32):
    return jax.ShapeDtypeStruct(shape, dtype)


def cost(flops, moved):
    return pl.CostEstimate(flops=flops, bytes_accessed=moved, transcendentals=0)


def split(x):
    high = x.astype(BF)
    return high, (x - high.astype(F32)).astype(BF)


def stacked_split(x):
    return jnp.concatenate(split(x), axis=0)


def dot(a, b):
    return lax.dot_general(a, b, (((1,), (0,)), ((), ())), preferred_element_type=F32)


def whole(shape):
    return pl.BlockSpec(shape, lambda *_: (0,) * len(shape))


def exponent_of(peak):
    return jnp.floor(jnp.log(jnp.maximum(peak, 1e-30)) * (1.0 / math.log(2.0))) - 14.0


def code(x):
    return jnp.clip(jnp.floor(x + 0.5), -32767.0, 32767.0).astype(jnp.int32).astype(jnp.int16)


def peak_of(x):
    return jnp.max(jnp.abs(x), axis=(0, 1), keepdims=True)


def exponent_tile(rows, lanes):
    rows = [jnp.broadcast_to(r, (1, lanes)) for r in rows]
    rows.append(jnp.zeros((16 - len(rows), lanes), F32))
    return jnp.concatenate(rows, axis=0).astype(jnp.int32).astype(jnp.int16)


def lanes_sum(x):
    total = x[:, :128]
    for i in range(1, x.shape[1] // 128):
        total = total + x[:, i * 128 : (i + 1) * 128]
    return jnp.sum(total, axis=0, keepdims=True)


def total(rows):
    return jnp.sum(rows, axis=(0, 1), keepdims=True)


def transform_body(up_ref, table_ref, inverse_ref, mine_ref, other_ref, sums, exponents):
    me = lax.axis_index("core")
    index = jnp.broadcast_to(inverse_ref[...], (64, 128))
    table = jnp.concatenate([table_ref[...].astype(F32)] * 8, axis=1)
    table = jnp.broadcast_to(table[:, None, :], (8, 8, 256)).reshape(64, 256)
    shot = lax.broadcasted_iota(jnp.int32, (64, 256), 0) % 8
    table = jnp.where(shot == lax.broadcasted_iota(jnp.int32, (64, 256), 1) // 32, table, 0.0).astype(BF)

    def step(block, carry):
        chip, core, first = block // 4, block // 2 % 2, block % 2 * 2
        largest = jnp.zeros((64, 128), F32)
        for pair in range(8):
            part, row = first + pair // 4, pair % 4 * 16
            x = [up_ref[chip, part, core, row + h * 8 : row + h * 8 + 8].reshape(256, 128) for h in range(2)]
            both = dot(table, jnp.concatenate(x, axis=1))
            for h in range(2):
                y = jnp.take_along_axis(both[:, h * 128 : h * 128 + 128], index, axis=1)
                largest = jnp.maximum(largest, jnp.abs(y))
                at = pair // 4 * 64 + row + h * 8
                for fc in range(8):
                    sums[fc, at : at + 8, :] = y[fc * 8 : fc * 8 + 8]
        exponent = exponent_of(peak_of(largest))
        scale = jnp.exp2(-exponent)
        exponents[pl.ds(block, 1), :] = jnp.broadcast_to(exponent, (1, 128))
        rows = pl.multiple_of(block * 64, 64)
        for fc in range(8):
            turned = sums[fc].T * scale
            at = pl.ds(rows + (fc % 2) * 32, 32)
            for x in range(2):
                lower, upper = (turned[x * 64 + c * 32 : x * 64 + c * 32 + 32] for c in range(2))
                mine_ref[x * 4 + fc // 2, at, :] = code(jnp.where(me == 0, lower, upper))
                other_ref[x * 4 + fc // 2, at, :] = code(jnp.where(me == 0, upper, lower))
        return carry

    lax.fori_loop(0, 8, step, 0)
    coded = exponent_tile([exponents[i : i + 1, :] for i in range(8)], 128)
    for dest in range(8):
        mine_ref[dest, 512:528, :] = coded
        other_ref[dest, 512:528, :] = coded


def transform(up_time, table, inverse):
    return pl.pallas_call(
        transform_body,
        in_specs=[HELD] * 3,
        out_specs=[HELD] * 2,
        out_shape=[struct((8, 528, 128), jnp.int16)] * 2,
        scratch_shapes=[pltpu.VMEM((8, 128, 128), F32), pltpu.VMEM((8, 128), F32)],
        compiler_params=SMALL,
        cost_estimate=cost(600_000_000, 10_000_000),
        name="transform",
    )(up_time.reshape(2, 4, 2, 64, 32, 128), table, inverse)


def merge_body(mine_ref, other_ref, *out_refs):
    chip = lax.axis_index("xl") * 4 + lax.axis_index("z")
    scales = [jnp.exp2(r[0, 512:528, :].astype(F32)) for r in (mine_ref, other_ref)]
    exponents = []
    for block in range(8):
        rows = slice(block * 64, block * 64 + 64)
        sums, largest = [], jnp.zeros((64, 128), F32)
        for i in range(8):
            dest = chip ^ i
            mine = mine_ref[dest, rows, :].astype(F32) * scales[0][block : block + 1]
            sums.append(mine + other_ref[dest, rows, :].astype(F32) * scales[1][block : block + 1])
            largest = jnp.maximum(largest, jnp.abs(sums[-1]))
        exponents.append(exponent_of(peak_of(largest)))
        scale = jnp.exp2(-exponents[-1])
        for i in range(8):
            out_refs[i][rows, :] = code(sums[i] * scale)
    coded = exponent_tile(exponents, 128)
    for out_ref in out_refs:
        out_ref[512:528, :] = coded


def merge(pieces, other):
    return pl.pallas_call(
        merge_body,
        out_shape=[struct((528, 128), jnp.int16)] * 8,
        compiler_params=SMALL,
        cost_estimate=cost(10_000_000, 3_000_000),
        name="merge",
    )(pieces, other)


def collect_body(*refs):
    in_refs, out_ref = refs[:-1], refs[-1]
    scales = [jnp.exp2(ref[512:528, :].astype(F32)) for ref in in_refs]
    for block in range(8):
        summed = jnp.zeros((64, 128), F32)
        for ref, scale in zip(in_refs, scales):
            piece = ref[block * 64 : block * 64 + 64, :].astype(F32)
            summed = summed + piece * scale[block : block + 1]
        out_ref[:, block * 128 : block * 128 + 128] = summed


def collect(received):
    return pl.pallas_call(
        collect_body,
        out_shape=struct((64, 1024)),
        compiler_params=SMALL,
        cost_estimate=cost(5_000_000, 2_000_000),
        name="collect",
    )(*received)


def code_down_body(in_ref, out_ref, coded, sent):
    for f in range(F):
        field = in_ref[f].reshape(128, 128)
        exponent = exponent_of(peak_of(field))
        coded[f, 0:128, :] = code(field * jnp.exp2(-exponent))
        coded[f, 128:144, :] = exponent_tile([exponent], 128)
    copies = [
        pltpu.make_async_copy(coded, out_ref.at[pl.ds(i * F, F)], sent.at[i]) for i in range(16)
    ]
    for copy in copies:
        copy.start()
    for copy in copies:
        copy.wait()


def code_down(downgoing):
    return pl.pallas_call(
        code_down_body,
        in_specs=[HELD],
        out_specs=pl.BlockSpec(memory_space=pl.ANY),
        out_shape=struct((64, 144, 128), jnp.int16),
        scratch_shapes=[pltpu.VMEM((F, 144, 128), jnp.int16), pltpu.SemaphoreType.DMA((16,))],
        compiler_params=FULL,
        cost_estimate=cost(1_000_000, 3_000_000),
        name="code_down",
    )(downgoing)


def adjoint_step(down_ref, both, nodes=slice(None)):
    sums = []
    for c in range(2):
        first = dot(both, down_ref[0, c, :, nodes])
        sums.append(first[:64] + first[64:] + dot(both[:64], down_ref[1, c, :, nodes]))
    real = sums[0][:32] + sums[1][32:]
    imaginary = sums[0][32:] - sums[1][:32]
    return jnp.concatenate([real, imaginary], axis=0)


def forward_step(down_ref, both, shots):
    sums = []
    for c in range(2):
        first = dot(down_ref[0, c, shots, :], both) + dot(down_ref[1, c, shots, :], both)
        sums.append((first[:, :64] + first[:, 64:]).T)
    real = sums[0][:32] - sums[1][32:]
    imaginary = sums[0][32:] + sums[1][:32]
    return jnp.concatenate([real, imaginary], axis=0)


def side_split(field):
    return jnp.concatenate(split(field.T), axis=1)


def pack(field, out_ref, first, scale=None):
    turned = field.T
    for k in range(8):
        piece = turned[k * 32 : k * 32 + 32]
        piece = jnp.concatenate([piece[:16], piece[16:]], axis=1)
        out_ref[first + k, 0:16, :] = piece if scale is None else code(piece * scale)


def unpack(in_ref, first):
    pieces = [in_ref[first + k, 0:16, :].astype(F32) for k in range(4)]
    if in_ref.dtype == jnp.int16:
        for k in range(4):
            scale = jnp.exp2(in_ref[first + k, 16:32, :].astype(F32)[0:1])
            pieces[k] = pieces[k] * scale
    rows = []
    for c in range(2):
        for half in range(2):
            at = half * 64 + c * 32
            rows.append(jnp.concatenate([p[:, at : at + 32] for p in pieces], axis=1))
    return jnp.concatenate(rows, axis=0)


def symmetric(field, in_ref, first):
    mirrored = jnp.concatenate([unpack(in_ref, first), unpack(in_ref, first + 4)], axis=1)
    return (field + mirrored) * 0.5


def decode_body(mine_ref, other_ref, down_ref):
    me = lax.axis_index("core")
    for n in range(8):
        lanes = slice(n * 128, n * 128 + 128)
        for source, core in ((mine_ref, me), (other_ref, 1 - me)):
            for x in range(2):
                for z in range(4):
                    scale = jnp.exp2(source[x, n % 2, n // 2, z, 128:144, :].astype(F32))[0:1]
                    first = x * 512 + core * 256 + z * 64
                    rows = pl.ds(pl.multiple_of(first, 64), 64)
                    for c in range(2):
                        field = source[x, n % 2, n // 2, z, c * 64 : c * 64 + 64, :].astype(F32) * scale
                        high, low = split(field)
                        down_ref[0, c, rows, lanes] = high
                        down_ref[1, c, rows, lanes] = low


def decode(mine, other):
    return pl.pallas_call(
        decode_body,
        in_specs=[HELD] * 2,
        out_specs=HELD,
        out_shape=struct((2, 2, 1024, 1024), BF),
        compiler_params=SMALL,
        cost_estimate=cost(20_000_000, 13_000_000),
        name="decode",
    )(mine.reshape(2, 2, 4, 4, 144, 128), other.reshape(2, 2, 4, 4, 144, 128))


def first_adjoint_body(data_ref, down_ref, field_ref, pieces_ref):
    both = stacked_split(data_ref[...])
    for i in range(4):
        at = slice(i * 256, i * 256 + 256)
        field = adjoint_step(down_ref, both, at)
        field_ref[:, at] = field
        pack(field, pieces_ref, i * 8)


def first_adjoint(data, down):
    return pl.pallas_call(
        first_adjoint_body,
        in_specs=[HELD] * 2,
        out_specs=[HELD] * 2,
        out_shape=[struct((64, 1024)), struct((32, 16, 128))],
        compiler_params=SMALL,
        cost_estimate=cost(800_000_000, 9_000_000),
        name="first_adjoint",
    )(data, down)


def second_body(field_ref, in_ref, down_ref, gradient_ref, image_ref, again_ref, out_ref, side, both):
    blocks = [slice(i * 256, i * 256 + 256) for i in range(4)]
    for i, at in enumerate(blocks):
        gradient = symmetric(field_ref[:, at], in_ref, i * 8)
        gradient_ref[:, at] = gradient
        side[at, :] = side_split(gradient)
    for at in blocks:
        image = forward_step(down_ref, side[...], at)
        image_ref[:, at] = image
        both[:, at] = stacked_split(image)
    gradient, image = gradient_ref[...], image_ref[...]
    for at in blocks:
        again_ref[:, at] = adjoint_step(down_ref, both[...], at)
    exponent = exponent_of(peak_of(again_ref[...]))
    rows = [exponent]
    for row in (lanes_sum(gradient * gradient), lanes_sum(image * image)):
        rows.append(exponent_of(peak_of(row)))
        scaled = row * jnp.exp2(-rows[-1])
        rows.append(jnp.minimum(jnp.floor(scaled), 32767.0))
        rows.append(jnp.minimum(jnp.floor((scaled - rows[-1]) * 32768.0), 32767.0))
    tile = exponent_tile(rows, 128)
    for i, at in enumerate(blocks):
        pack(again_ref[:, at], out_ref, i * 8, jnp.exp2(-exponent))
    for k in range(32):
        out_ref[k, 16:32, :] = tile


def second(field, received, down):
    return pl.pallas_call(
        second_body,
        in_specs=[HELD] * 3,
        out_specs=[HELD] * 4,
        out_shape=[struct((64, 1024))] * 3 + [struct((32, 32, 128), jnp.int16)],
        scratch_shapes=[pltpu.VMEM((1024, 128), BF), pltpu.VMEM((128, 1024), BF)],
        compiler_params=SMALL,
        cost_estimate=cost(1_600_000_000, 18_000_000),
        name="second",
    )(field, received, down)


def first_step(in_ref):
    sums = [jnp.zeros((1, 128), F32)] * 2
    for k in range(32):
        tile = in_ref[k, 16:32, :].astype(F32)
        for i in range(2):
            at = 1 + 3 * i
            value = tile[at + 1 : at + 2] + tile[at + 2 : at + 3] * (1.0 / 32768.0)
            sums[i] = sums[i] + value * jnp.exp2(tile[at : at + 1])
    return total(sums[0]), total(sums[1])


def change_body(
    gradient_ref, field_ref, image_ref, in_ref, down_ref, again_ref, change_ref, out_ref, side
):
    blocks = [slice(i * 256, i * 256 + 256) for i in range(4)]
    norm, curvature = first_step(in_ref)
    step = norm / curvature
    for i, at in enumerate(blocks):
        again = symmetric(field_ref[:, at], in_ref, i * 8)
        again_ref[:, at] = again
        side[at, :] = side_split(again)
    for at in blocks:
        change_ref[:, at] = image_ref[:, at] - step * forward_step(down_ref, side[...], at)
    gradient = gradient_ref[...] - step * again_ref[...]
    change = change_ref[...]
    rows = [gradient * gradient, change * change, change * image_ref[...]]
    rows = [lanes_sum(row) for row in rows] + [jnp.zeros((5, 128), F32)]
    sums = jnp.concatenate(rows, axis=0)
    for i in range(32):
        out_ref[i] = sums


def changed(gradient, field, image, received, down):
    return pl.pallas_call(
        change_body,
        in_specs=[HELD] * 5,
        out_specs=[HELD] * 3,
        out_shape=[struct((64, 1024)), struct((64, 1024)), struct((32, 8, 128))],
        scratch_shapes=[pltpu.VMEM((1024, 128), BF)],
        compiler_params=SMALL,
        cost_estimate=cost(800_000_000, 9_000_000),
        name="change",
    )(gradient, field, image, received, down)


def side_by_side(field):
    turned = field.T
    return jnp.concatenate([turned[:512], turned[512:]], axis=1)


def update_body(
    data_ref, gradient_ref, again_ref, image_ref, change_ref, in_ref, sums_ref, out_ref
):
    norm, curvature = first_step(in_ref)
    step = norm / curvature
    rows = jnp.sum(sums_ref[...], axis=0)
    new_norm, change_change, change_image = (total(rows[i : i + 1]) for i in range(3))
    beta = new_norm / norm
    new_step = new_norm / (change_change + 2.0 * beta * change_image + beta * beta * curvature)
    gradient, image = gradient_ref[...], image_ref[...]
    direction = (gradient - step * again_ref[...]) + beta * gradient
    result = step * gradient + new_step * direction
    left = data_ref[...] - step * image - new_step * (change_ref[...] + beta * image)
    exponents = [exponent_of(peak_of(result)), exponent_of(peak_of(left))]
    own = lax.axis_index("xl") * 2 + lax.axis_index("core")
    coded = code(pltpu.roll(side_by_side(result * jnp.exp2(-exponents[0])), own * 32, 1))
    turned = (left * jnp.exp2(-exponents[1])).T
    tile = exponent_tile(exponents, 128)
    for dest in range(8):
        out_ref[dest, 0:512, :] = coded
        for core in range(2):
            at = (dest % 2 * 2 + core) * 256 + dest // 2 * 64
            piece = jnp.concatenate([turned[at : at + 32], turned[at + 32 : at + 64]], axis=1)
            out_ref[dest, 512 + core * 32 : 544 + core * 32, :] = code(piece)
        out_ref[dest, 576:592, :] = tile


def updated(data, gradient, again, image, change, received, sums):
    return pl.pallas_call(
        update_body,
        out_shape=struct((8, 592, 128), jnp.int16),
        compiler_params=SMALL,
        cost_estimate=cost(5_000_000, 3_000_000),
        name="update",
    )(data, gradient, again, image, change, received, sums)


def place(f, first_ref, second_ref, core, reflectivity_ref, residual_ref):
    refs = [ref.at[f, x] for x in range(2) for ref in (first_ref, second_ref)]
    scales = [jnp.exp2(ref[576:592, :].astype(F32)) for ref in refs]
    owner = lax.broadcasted_iota(jnp.int32, (64, 128), 1) // 32
    spread = scales[3][0:1]
    for k in range(3):
        spread = jnp.where(owner[0:1] == k, scales[k][0:1], spread)
    for j in range(8):
        parts = [ref[j * 64 : j * 64 + 64, :].astype(F32) for ref in refs]
        for q in range(4):
            mixed = parts[(3 - q) % 4]
            for b in range(3):
                mixed = jnp.where(owner == b, parts[(b - q) % 4], mixed)
            if q:
                mixed = pltpu.roll(mixed, 128 - 32 * q, 1)
            first = q // 2 * 512 + j * 64
            reflectivity_ref[0, q % 2, first : first + 64, :] = mixed * spread
    rows = slice(512 + core * 32, 544 + core * 32)
    pieces = [ref[rows, :].astype(F32) * scale[1:2] for ref, scale in zip(refs, scales)]
    for c in range(2):
        for half in range(2):
            at = half * 64 + c * 32
            row = jnp.concatenate([p[:, at : at + 32] for p in pieces], axis=1)
            residual_ref[0, c, half * 32 : half * 32 + 32, :] = row


def finish_body(mine_ref, other_ref, reflectivity_ref, residual_ref):
    f = pl.program_id(0)
    me = lax.axis_index("core")

    @pl.when(me == 0)
    def _():
        place(f, mine_ref, other_ref, 0, reflectivity_ref, residual_ref)

    @pl.when(me == 1)
    def _():
        place(f, other_ref, mine_ref, 1, reflectivity_ref, residual_ref)


def finish(mine, other):
    return pl.pallas_call(
        finish_body,
        grid=(F,),
        in_specs=[HELD] * 2,
        out_specs=[
            pl.BlockSpec((1, 2, 1024, 128), lambda f: (f, 0, 0, 0)),
            pl.BlockSpec((1, 2, 64, 128), lambda f: (f, 0, 0, 0)),
        ],
        out_shape=[struct((F, 2, 1024, 128)), struct((F, 2, 64, 128))],
        compiler_params=SMALL,
        cost_estimate=cost(10_000_000, 7_000_000),
        name="finish",
    )(mine.reshape(F, 2, 592, 128), other.reshape(F, 2, 592, 128))


def swap_cores(x):
    return lax.ppermute(x, "core", [(0, 1), (1, 0)])


def shards(up_time, downgoing, freq_idx, node_map):
    mine = lax.all_to_all(code_down(downgoing), ALL_CHIPS, 0, 0, tiled=True)
    count = up_time.shape[1]
    table = local_table(freq_idx, lax.axis_index(SHOT) * count, count)
    slots = jnp.arange(128, dtype=jnp.int32)
    inverse = jnp.sum(jnp.where(node_map[:, None] == slots[None, :], slots[:, None], 0), axis=0)
    pieces, others = transform(up_time, table, inverse[None, :])
    pieces = merge(pieces, swap_cores(others))
    received = [lax.ppermute(pieces[i], CHIPS, [(k, k ^ i) for k in range(8)]) for i in ORDER]
    mine, received[:4] = lax.optimization_barrier((mine, received[:4]))
    down = decode(mine, swap_cores(mine))
    received[4:], down = lax.optimization_barrier((received[4:], down))
    data = collect([pieces[0], *received])

    field, pieces = first_adjoint(data, down)
    received = lax.all_to_all(pieces, PLANE, 0, 0, tiled=True)
    gradient, image, field, pieces = second(field, received, down)
    received = lax.all_to_all(pieces, PLANE, 0, 0, tiled=True)
    again, change, sums = changed(gradient, field, image, received, down)
    sums = lax.all_to_all(sums, PLANE, 0, 0, tiled=True)
    pieces = updated(data, gradient, again, image, change, received, sums)
    mine = lax.all_to_all(pieces, ("z", "xl"), 0, 0, tiled=True)
    return tuple(finish(mine, swap_cores(mine)))


def solution(mesh):
    fine = Mesh(mesh.devices.reshape(2, 4, 2, 4, 2), SHOT + NODE)
    return jax.shard_map(
        shards,
        mesh=fine,
        in_specs=(P(None, SHOT, NODE), P(None, None, SHOT, NODE), P(), P(NODE)),
        out_specs=(P(None, None, None, NODE), P(None, None, SHOT, NODE)),
        check_vma=False,
    )
```

```python
import math

import jax
import jax.numpy as jnp
from jax import lax
from jax.experimental import pallas as pl
from jax.experimental.pallas import tpu as pltpu
from jax.sharding import Mesh, PartitionSpec as P

NODES = 1024
NT = 512
F = 4
SHOT = ("xl", "z", "core")
NODE = ("y", "xh")
CHIPS = ("xl", "z")
ORDER = (6, 7, 5, 2, 3, 1, 4)
ALL_CHIPS = ("xl", "xh", "y", "z")
PLANE = ("y", "xh", "xl", "core")
BF = jnp.bfloat16
F32 = jnp.float32
HELD = pl.BlockSpec(memory_space=pltpu.VMEM)
SMALL = pltpu.CompilerParams(vmem_limit_bytes=16 * 1024 * 1024)
FULL = pltpu.CompilerParams(vmem_limit_bytes=58 * 1024 * 1024)


def local_table(freq_idx, first, count):
    sample = first + jnp.arange(count, dtype=jnp.int32)
    product = freq_idx[:, None] * sample[None, :] % NT
    angle = product.astype(F32) * (2.0 * math.pi / NT)
    stacked = jnp.stack([jnp.cos(angle), -jnp.sin(angle)], axis=1)
    return stacked.reshape(2 * F, count).astype(BF)


def struct(shape, dtype=F32):
    return jax.ShapeDtypeStruct(shape, dtype)


def cost(flops, moved):
    return pl.CostEstimate(flops=flops, bytes_accessed=moved, transcendentals=0)


def split(x):
    high = x.astype(BF)
    return high, (x - high.astype(F32)).astype(BF)


def stacked_split(x):
    return jnp.concatenate(split(x), axis=0)


def dot(a, b):
    return lax.dot_general(a, b, (((1,), (0,)), ((), ())), preferred_element_type=F32)


def whole(shape):
    return pl.BlockSpec(shape, lambda *_: (0,) * len(shape))


def exponent_of(peak):
    return jnp.floor(jnp.log(jnp.maximum(peak, 1e-30)) * (1.0 / math.log(2.0))) - 14.0


def code(x):
    return jnp.clip(jnp.floor(x + 0.5), -32767.0, 32767.0).astype(jnp.int32).astype(jnp.int16)


def peak_of(x):
    return jnp.max(jnp.abs(x), axis=(0, 1), keepdims=True)


def exponent_tile(rows, lanes):
    rows = [jnp.broadcast_to(r, (1, lanes)) for r in rows]
    rows.append(jnp.zeros((16 - len(rows), lanes), F32))
    return jnp.concatenate(rows, axis=0).astype(jnp.int32).astype(jnp.int16)


def lanes_sum(x):
    total = x[:, :128]
    for i in range(1, x.shape[1] // 128):
        total = total + x[:, i * 128 : (i + 1) * 128]
    return jnp.sum(total, axis=0, keepdims=True)


def total(rows):
    return jnp.sum(rows, axis=(0, 1), keepdims=True)


def transform_body(up_ref, table_ref, inverse_ref, mine_ref, other_ref, sums, exponents):
    me = lax.axis_index("core")
    index = jnp.broadcast_to(inverse_ref[...], (64, 128))
    table = jnp.concatenate([table_ref[...].astype(F32)] * 8, axis=1)
    table = jnp.broadcast_to(table[:, None, :], (8, 8, 256)).reshape(64, 256)
    shot = lax.broadcasted_iota(jnp.int32, (64, 256), 0) % 8
    table = jnp.where(shot == lax.broadcasted_iota(jnp.int32, (64, 256), 1) // 32, table, 0.0).astype(BF)

    def step(block, carry):
        chip, core, first = block // 4, block // 2 % 2, block % 2 * 2
        largest = jnp.zeros((64, 128), F32)
        for pair in range(8):
            part, row = first + pair // 4, pair % 4 * 16
            x = [up_ref[chip, part, core, row + h * 8 : row + h * 8 + 8].reshape(256, 128) for h in range(2)]
            both = dot(table, jnp.concatenate(x, axis=1))
            for h in range(2):
                y = jnp.take_along_axis(both[:, h * 128 : h * 128 + 128], index, axis=1)
                largest = jnp.maximum(largest, jnp.abs(y))
                at = pair // 4 * 64 + row + h * 8
                for fc in range(8):
                    sums[fc, at : at + 8, :] = y[fc * 8 : fc * 8 + 8]
        exponent = exponent_of(peak_of(largest))
        scale = jnp.exp2(-exponent)
        exponents[pl.ds(block, 1), :] = jnp.broadcast_to(exponent, (1, 128))
        rows = pl.multiple_of(block * 64, 64)
        for fc in range(8):
            turned = sums[fc].T * scale
            at = pl.ds(rows + (fc % 2) * 32, 32)
            for x in range(2):
                lower, upper = (turned[x * 64 + c * 32 : x * 64 + c * 32 + 32] for c in range(2))
                mine_ref[x * 4 + fc // 2, at, :] = code(jnp.where(me == 0, lower, upper))
                other_ref[x * 4 + fc // 2, at, :] = code(jnp.where(me == 0, upper, lower))
        return carry

    lax.fori_loop(0, 8, step, 0)
    coded = exponent_tile([exponents[i : i + 1, :] for i in range(8)], 128)
    for dest in range(8):
        mine_ref[dest, 512:528, :] = coded
        other_ref[dest, 512:528, :] = coded


def transform(up_time, table, inverse):
    return pl.pallas_call(
        transform_body,
        in_specs=[HELD] * 3,
        out_specs=[HELD] * 2,
        out_shape=[struct((8, 528, 128), jnp.int16)] * 2,
        scratch_shapes=[pltpu.VMEM((8, 128, 128), F32), pltpu.VMEM((8, 128), F32)],
        compiler_params=SMALL,
        cost_estimate=cost(600_000_000, 10_000_000),
        name="transform",
    )(up_time.reshape(2, 4, 2, 64, 32, 128), table, inverse)


def merge_body(mine_ref, other_ref, *out_refs):
    chip = lax.axis_index("xl") * 4 + lax.axis_index("z")
    scales = [jnp.exp2(r[0, 512:528, :].astype(F32)) for r in (mine_ref, other_ref)]
    exponents = []
    for block in range(8):
        rows = slice(block * 64, block * 64 + 64)
        sums, largest = [], jnp.zeros((64, 128), F32)
        for i in range(8):
            dest = chip ^ i
            mine = mine_ref[dest, rows, :].astype(F32) * scales[0][block : block + 1]
            sums.append(mine + other_ref[dest, rows, :].astype(F32) * scales[1][block : block + 1])
            largest = jnp.maximum(largest, jnp.abs(sums[-1]))
        exponents.append(exponent_of(peak_of(largest)))
        scale = jnp.exp2(-exponents[-1])
        for i in range(8):
            out_refs[i][rows, :] = code(sums[i] * scale)
    coded = exponent_tile(exponents, 128)
    for out_ref in out_refs:
        out_ref[512:528, :] = coded


def merge(pieces, other):
    return pl.pallas_call(
        merge_body,
        out_shape=[struct((528, 128), jnp.int16)] * 8,
        compiler_params=SMALL,
        cost_estimate=cost(10_000_000, 3_000_000),
        name="merge",
    )(pieces, other)


def collect_body(*refs):
    in_refs, out_ref = refs[:-1], refs[-1]
    scales = [jnp.exp2(ref[512:528, :].astype(F32)) for ref in in_refs]
    for block in range(8):
        summed = jnp.zeros((64, 128), F32)
        for ref, scale in zip(in_refs, scales):
            piece = ref[block * 64 : block * 64 + 64, :].astype(F32)
            summed = summed + piece * scale[block : block + 1]
        out_ref[:, block * 128 : block * 128 + 128] = summed


def collect(received):
    return pl.pallas_call(
        collect_body,
        out_shape=struct((64, 1024)),
        compiler_params=SMALL,
        cost_estimate=cost(5_000_000, 2_000_000),
        name="collect",
    )(*received)


def code_down_body(in_ref, out_ref, coded, sent):
    for f in range(F):
        field = in_ref[f].reshape(128, 128)
        exponent = exponent_of(peak_of(field))
        coded[f, 0:128, :] = code(field * jnp.exp2(-exponent))
        coded[f, 128:144, :] = exponent_tile([exponent], 128)
    copies = [
        pltpu.make_async_copy(coded, out_ref.at[pl.ds(i * F, F)], sent.at[i]) for i in range(16)
    ]
    for copy in copies:
        copy.start()
    for copy in copies:
        copy.wait()


def code_down(downgoing):
    return pl.pallas_call(
        code_down_body,
        in_specs=[HELD],
        out_specs=pl.BlockSpec(memory_space=pl.ANY),
        out_shape=struct((64, 144, 128), jnp.int16),
        scratch_shapes=[pltpu.VMEM((F, 144, 128), jnp.int16), pltpu.SemaphoreType.DMA((16,))],
        compiler_params=FULL,
        cost_estimate=cost(1_000_000, 3_000_000),
        name="code_down",
    )(downgoing)


def adjoint_step(down_ref, both, nodes=slice(None)):
    sums = []
    for c in range(2):
        first = dot(both, down_ref[0, c, :, nodes])
        sums.append(first[:64] + first[64:] + dot(both[:64], down_ref[1, c, :, nodes]))
    real = sums[0][:32] + sums[1][32:]
    imaginary = sums[0][32:] - sums[1][:32]
    return jnp.concatenate([real, imaginary], axis=0)


def forward_step(down_ref, both, shots):
    sums = []
    for c in range(2):
        first = dot(down_ref[0, c, shots, :], both)
        first = first[:, :64] + first[:, 64:] + dot(down_ref[1, c, shots, :], both[:, :64])
        sums.append(first.T)
    real = sums[0][:32] - sums[1][32:]
    imaginary = sums[0][32:] + sums[1][:32]
    return jnp.concatenate([real, imaginary], axis=0)


def side_split(field):
    return jnp.concatenate(split(field.T), axis=1)


def pack(field, out_ref, first, scale=None):
    turned = field.T
    for k in range(8):
        piece = turned[k * 32 : k * 32 + 32]
        piece = jnp.concatenate([piece[:16], piece[16:]], axis=1)
        out_ref[first + k, 0:16, :] = piece if scale is None else code(piece * scale)


def unpack(in_ref, first):
    pieces = [in_ref[first + k, 0:16, :].astype(F32) for k in range(4)]
    if in_ref.dtype == jnp.int16:
        for k in range(4):
            scale = jnp.exp2(in_ref[first + k, 16:32, :].astype(F32)[0:1])
            pieces[k] = pieces[k] * scale
    rows = []
    for c in range(2):
        for half in range(2):
            at = half * 64 + c * 32
            rows.append(jnp.concatenate([p[:, at : at + 32] for p in pieces], axis=1))
    return jnp.concatenate(rows, axis=0)


def symmetric(field, in_ref, first):
    mirrored = jnp.concatenate([unpack(in_ref, first), unpack(in_ref, first + 4)], axis=1)
    return (field + mirrored) * 0.5


def decode_body(mine_ref, other_ref, down_ref):
    me = lax.axis_index("core")
    for n in range(8):
        lanes = slice(n * 128, n * 128 + 128)
        for source, core in ((mine_ref, me), (other_ref, 1 - me)):
            for x in range(2):
                for z in range(4):
                    scale = jnp.exp2(source[x, n % 2, n // 2, z, 128:144, :].astype(F32))[0:1]
                    first = x * 512 + core * 256 + z * 64
                    rows = pl.ds(pl.multiple_of(first, 64), 64)
                    for c in range(2):
                        field = source[x, n % 2, n // 2, z, c * 64 : c * 64 + 64, :].astype(F32) * scale
                        high, low = split(field)
                        down_ref[0, c, rows, lanes] = high
                        down_ref[1, c, rows, lanes] = low


def decode(mine, other):
    return pl.pallas_call(
        decode_body,
        in_specs=[HELD] * 2,
        out_specs=HELD,
        out_shape=struct((2, 2, 1024, 1024), BF),
        compiler_params=SMALL,
        cost_estimate=cost(20_000_000, 13_000_000),
        name="decode",
    )(mine.reshape(2, 2, 4, 4, 144, 128), other.reshape(2, 2, 4, 4, 144, 128))


def first_adjoint_body(data_ref, down_ref, field_ref, pieces_ref):
    both = stacked_split(data_ref[...])
    for i in range(4):
        at = slice(i * 256, i * 256 + 256)
        field = adjoint_step(down_ref, both, at)
        field_ref[:, at] = field
        pack(field, pieces_ref, i * 8)


def first_adjoint(data, down):
    return pl.pallas_call(
        first_adjoint_body,
        in_specs=[HELD] * 2,
        out_specs=[HELD] * 2,
        out_shape=[struct((64, 1024)), struct((32, 16, 128))],
        compiler_params=SMALL,
        cost_estimate=cost(800_000_000, 9_000_000),
        name="first_adjoint",
    )(data, down)


def second_body(field_ref, in_ref, down_ref, gradient_ref, image_ref, again_ref, out_ref, side, both):
    blocks = [slice(i * 256, i * 256 + 256) for i in range(4)]
    for i, at in enumerate(blocks):
        gradient = symmetric(field_ref[:, at], in_ref, i * 8)
        gradient_ref[:, at] = gradient
        side[at, :] = side_split(gradient)
    for at in blocks:
        image = forward_step(down_ref, side[...], at)
        image_ref[:, at] = image
        both[:, at] = stacked_split(image)
    gradient, image = gradient_ref[...], image_ref[...]
    for at in blocks:
        again_ref[:, at] = adjoint_step(down_ref, both[...], at)
    exponent = exponent_of(peak_of(again_ref[...]))
    rows = [exponent]
    for row in (lanes_sum(gradient * gradient), lanes_sum(image * image)):
        rows.append(exponent_of(peak_of(row)))
        scaled = row * jnp.exp2(-rows[-1])
        rows.append(jnp.minimum(jnp.floor(scaled), 32767.0))
        rows.append(jnp.minimum(jnp.floor((scaled - rows[-1]) * 32768.0), 32767.0))
    tile = exponent_tile(rows, 128)
    for i, at in enumerate(blocks):
        pack(again_ref[:, at], out_ref, i * 8, jnp.exp2(-exponent))
    for k in range(32):
        out_ref[k, 16:32, :] = tile


def second(field, received, down):
    return pl.pallas_call(
        second_body,
        in_specs=[HELD] * 3,
        out_specs=[HELD] * 4,
        out_shape=[struct((64, 1024))] * 3 + [struct((32, 32, 128), jnp.int16)],
        scratch_shapes=[pltpu.VMEM((1024, 128), BF), pltpu.VMEM((128, 1024), BF)],
        compiler_params=SMALL,
        cost_estimate=cost(1_600_000_000, 18_000_000),
        name="second",
    )(field, received, down)


def first_step(in_ref):
    sums = [jnp.zeros((1, 128), F32)] * 2
    for k in range(32):
        tile = in_ref[k, 16:32, :].astype(F32)
        for i in range(2):
            at = 1 + 3 * i
            value = tile[at + 1 : at + 2] + tile[at + 2 : at + 3] * (1.0 / 32768.0)
            sums[i] = sums[i] + value * jnp.exp2(tile[at : at + 1])
    return total(sums[0]), total(sums[1])


def change_body(
    gradient_ref, field_ref, image_ref, in_ref, down_ref, again_ref, change_ref, out_ref, side
):
    blocks = [slice(i * 256, i * 256 + 256) for i in range(4)]
    norm, curvature = first_step(in_ref)
    step = norm / curvature
    for i, at in enumerate(blocks):
        again = symmetric(field_ref[:, at], in_ref, i * 8)
        again_ref[:, at] = again
        side[at, :] = side_split(again)
    for at in blocks:
        change_ref[:, at] = image_ref[:, at] - step * forward_step(down_ref, side[...], at)
    gradient = gradient_ref[...] - step * again_ref[...]
    change = change_ref[...]
    rows = [gradient * gradient, change * change, change * image_ref[...]]
    rows = [lanes_sum(row) for row in rows] + [jnp.zeros((5, 128), F32)]
    sums = jnp.concatenate(rows, axis=0)
    for i in range(32):
        out_ref[i] = sums


def changed(gradient, field, image, received, down):
    return pl.pallas_call(
        change_body,
        in_specs=[HELD] * 5,
        out_specs=[HELD] * 3,
        out_shape=[struct((64, 1024)), struct((64, 1024)), struct((32, 8, 128))],
        scratch_shapes=[pltpu.VMEM((1024, 128), BF)],
        compiler_params=SMALL,
        cost_estimate=cost(800_000_000, 9_000_000),
        name="change",
    )(gradient, field, image, received, down)


def side_by_side(field):
    turned = field.T
    return jnp.concatenate([turned[:512], turned[512:]], axis=1)


def update_body(
    data_ref, gradient_ref, again_ref, image_ref, change_ref, in_ref, sums_ref, out_ref
):
    norm, curvature = first_step(in_ref)
    step = norm / curvature
    rows = jnp.sum(sums_ref[...], axis=0)
    new_norm, change_change, change_image = (total(rows[i : i + 1]) for i in range(3))
    beta = new_norm / norm
    new_step = new_norm / (change_change + 2.0 * beta * change_image + beta * beta * curvature)
    gradient, image = gradient_ref[...], image_ref[...]
    direction = (gradient - step * again_ref[...]) + beta * gradient
    result = step * gradient + new_step * direction
    left = data_ref[...] - step * image - new_step * (change_ref[...] + beta * image)
    exponents = [exponent_of(peak_of(result)), exponent_of(peak_of(left))]
    own = lax.axis_index("xl") * 2 + lax.axis_index("core")
    coded = code(pltpu.roll(side_by_side(result * jnp.exp2(-exponents[0])), own * 32, 1))
    turned = (left * jnp.exp2(-exponents[1])).T
    tile = exponent_tile(exponents, 128)
    for dest in range(8):
        out_ref[dest, 0:512, :] = coded
        for core in range(2):
            at = (dest % 2 * 2 + core) * 256 + dest // 2 * 64
            piece = jnp.concatenate([turned[at : at + 32], turned[at + 32 : at + 64]], axis=1)
            out_ref[dest, 512 + core * 32 : 544 + core * 32, :] = code(piece)
        out_ref[dest, 576:592, :] = tile


def updated(data, gradient, again, image, change, received, sums):
    return pl.pallas_call(
        update_body,
        out_shape=struct((8, 592, 128), jnp.int16),
        compiler_params=SMALL,
        cost_estimate=cost(5_000_000, 3_000_000),
        name="update",
    )(data, gradient, again, image, change, received, sums)


def place(f, first_ref, second_ref, core, reflectivity_ref, residual_ref):
    refs = [ref.at[f, x] for x in range(2) for ref in (first_ref, second_ref)]
    scales = [jnp.exp2(ref[576:592, :].astype(F32)) for ref in refs]
    owner = lax.broadcasted_iota(jnp.int32, (64, 128), 1) // 32
    spread = scales[3][0:1]
    for k in range(3):
        spread = jnp.where(owner[0:1] == k, scales[k][0:1], spread)
    for j in range(8):
        parts = [ref[j * 64 : j * 64 + 64, :].astype(F32) for ref in refs]
        for q in range(4):
            mixed = parts[(3 - q) % 4]
            for b in range(3):
                mixed = jnp.where(owner == b, parts[(b - q) % 4], mixed)
            if q:
                mixed = pltpu.roll(mixed, 128 - 32 * q, 1)
            first = q // 2 * 512 + j * 64
            reflectivity_ref[0, q % 2, first : first + 64, :] = mixed * spread
    rows = slice(512 + core * 32, 544 + core * 32)
    pieces = [ref[rows, :].astype(F32) * scale[1:2] for ref, scale in zip(refs, scales)]
    for c in range(2):
        for half in range(2):
            at = half * 64 + c * 32
            row = jnp.concatenate([p[:, at : at + 32] for p in pieces], axis=1)
            residual_ref[0, c, half * 32 : half * 32 + 32, :] = row


def finish_body(mine_ref, other_ref, reflectivity_ref, residual_ref):
    f = pl.program_id(0)
    me = lax.axis_index("core")

    @pl.when(me == 0)
    def _():
        place(f, mine_ref, other_ref, 0, reflectivity_ref, residual_ref)

    @pl.when(me == 1)
    def _():
        place(f, other_ref, mine_ref, 1, reflectivity_ref, residual_ref)


def finish(mine, other):
    return pl.pallas_call(
        finish_body,
        grid=(F,),
        in_specs=[HELD] * 2,
        out_specs=[
            pl.BlockSpec((1, 2, 1024, 128), lambda f: (f, 0, 0, 0)),
            pl.BlockSpec((1, 2, 64, 128), lambda f: (f, 0, 0, 0)),
        ],
        out_shape=[struct((F, 2, 1024, 128)), struct((F, 2, 64, 128))],
        compiler_params=SMALL,
        cost_estimate=cost(10_000_000, 7_000_000),
        name="finish",
    )(mine.reshape(F, 2, 592, 128), other.reshape(F, 2, 592, 128))


def swap_cores(x):
    return lax.ppermute(x, "core", [(0, 1), (1, 0)])


def shards(up_time, downgoing, freq_idx, node_map):
    mine = lax.all_to_all(code_down(downgoing), ALL_CHIPS, 0, 0, tiled=True)
    count = up_time.shape[1]
    table = local_table(freq_idx, lax.axis_index(SHOT) * count, count)
    slots = jnp.arange(128, dtype=jnp.int32)
    inverse = jnp.sum(jnp.where(node_map[:, None] == slots[None, :], slots[:, None], 0), axis=0)
    pieces, others = transform(up_time, table, inverse[None, :])
    pieces = merge(pieces, swap_cores(others))
    received = [lax.ppermute(pieces[i], CHIPS, [(k, k ^ i) for k in range(8)]) for i in ORDER]
    mine, received[:4] = lax.optimization_barrier((mine, received[:4]))
    down = decode(mine, swap_cores(mine))
    received[4:], down = lax.optimization_barrier((received[4:], down))
    data = collect([pieces[0], *received])

    field, pieces = first_adjoint(data, down)
    received = lax.all_to_all(pieces, PLANE, 0, 0, tiled=True)
    gradient, image, field, pieces = second(field, received, down)
    received = lax.all_to_all(pieces, PLANE, 0, 0, tiled=True)
    again, change, sums = changed(gradient, field, image, received, down)
    sums = lax.all_to_all(sums, PLANE, 0, 0, tiled=True)
    pieces = updated(data, gradient, again, image, change, received, sums)
    mine = lax.all_to_all(pieces, ("z", "xl"), 0, 0, tiled=True)
    return tuple(finish(mine, swap_cores(mine)))


def solution(mesh):
    fine = Mesh(mesh.devices.reshape(2, 4, 2, 4, 2), SHOT + NODE)
    return jax.shard_map(
        shards,
        mesh=fine,
        in_specs=(P(None, SHOT, NODE), P(None, None, SHOT, NODE), P(), P(NODE)),
        out_specs=(P(None, None, None, NODE), P(None, None, SHOT, NODE)),
        check_vma=False,
    )
```
